32 devices in a mesh: expert: 4 (over x, core), dp: 8 (over z, y).
Axes of the slice: x: 2, y: 2, z: 4, core: 2. Of those that a mesh axis runs over, the one named last changes fastest.
Arguments:
- tokens: bfloat16 [4096, 1664], P(('expert', 'dp')), may hold values from -6 to 6
- expert_ids: int32 [4096, 2], P(('expert', 'dp')), may hold values from 0 to 7, as said below
- slot_ids: int32 [4096, 2], P(('expert', 'dp')), may hold values from 0 to 3, as said below
- dropped: int32 [4096, 2], P(('expert', 'dp')), may hold values from 0 to 1, as said below
- gates: float32 [4096, 2], P(('expert', 'dp')), may hold values from 0.1 to 1
- w_in: bfloat16 [8, 1664, 8192], P('expert', None, 'dp'), may hold values from -0.15625 to 0.15625
- w_out: bfloat16 [8, 8192, 1664], P('expert', 'dp'), may hold values from -0.0625 to 0.0625
- out_grad: bfloat16 [4096, 1664], P(('expert', 'dp')), may hold values from -6 to 6
Outputs:
- mixed: bfloat16 [4096, 1664], P(('expert', 'dp'))
- tok_grad: bfloat16 [4096, 1664], P(('expert', 'dp'))
- gate_grad: float32 [4096, 2], P(('expert', 'dp'))
- w_in_grad: float32 [8, 1664, 8192], P('expert', None, 'dp')
- w_out_grad: float32 [8, 8192, 1664], P('expert', 'dp')
The draws below stay inside these ranges and needn't reach their ends.
Inputs may be any that keep to these rules, and one draw needn't show every extreme that they name: `expert_ids`: the two experts of a token differ. `slot_ids`: choices are ranked in each block of 128 tokens by batch priority, all first choices before all second choices; a choice's slot is the number of higher-ranked choices of the same block to the same expert; it is dropped where that number is 4 or more, and its slot is then 0. Kept choices of one expert in one block have distinct slots. In every draw one expert is the first choice of at least 5 tokens of every block. `dropped`: 1 exactly where the slot count described for slot_ids reaches 4.
All inputs are finite; a program needn't handle non-finite values.
Results may differ from the reference program's by a relative error of at most 0.039.
Values may be sent and summed in bfloat16 or wider, within the bound.
No kernel may reach another device: no remote copies, remote signals or barrier semaphores. Data moves between devices by JAX's collectives and lax.ppermute only.
A program may use at most 128 MiB of HBM per device.

```python
import jax
import jax.numpy as jnp
from jax import lax

D = 1664
FF = 8192
CAP = 4
TOK_DEV = 128
EXPERTS = 8
TOKENS = 4096
N_DP = 8


def routing(key):
    base = jax.random.fold_in(key, 101)
    blocks = TOKENS // TOK_DEV
    key_hot, key_rank, key_first, key_second = jax.random.split(base, 4)
    favored = jax.random.randint(key_hot, (), 0, EXPERTS)

    def shuffle(sub_key):
        return jax.random.permutation(sub_key, TOK_DEV).astype(jnp.int32)
    priority = jax.vmap(shuffle)(jax.random.split(key_rank, blocks))
    random_first = jax.random.randint(key_first, (blocks, TOK_DEV), 0, EXPERTS)
    first = jnp.where(priority < CAP + 1, favored, random_first).astype(jnp.int32)
    offset = jax.random.randint(key_second, (blocks, TOK_DEV), 0, EXPERTS - 1)
    second = ((first + 1 + offset) % EXPERTS).astype(jnp.int32)
    chosen = jnp.stack([first, second], axis=-1)
    order_key = jnp.stack([priority, priority + TOK_DEV], axis=-1)
    flat_expert = chosen.reshape(blocks, 2 * TOK_DEV)
    flat_order = order_key.reshape(blocks, 2 * TOK_DEV)
    earlier = (flat_order[:, None, :] < flat_order[:, :, None]) & (flat_expert[:, None, :] == flat_expert[:, :, None])
    position = jnp.sum(earlier.astype(jnp.int32), axis=-1)
    overflow = (position >= CAP).astype(jnp.int32)
    slots = jnp.where(overflow > 0, 0, position).astype(jnp.int32)
    return (chosen.reshape(TOKENS, 2), slots.reshape(TOKENS, 2), overflow.reshape(TOKENS, 2))


def draw_expert_ids(key, part):
    return routing(key)[0]


def draw_slot_ids(key, part):
    return routing(key)[1]


def draw_dropped(key, part):
    return routing(key)[2]


def levels(own_key, shape, pieces, low, largest):
    gain = 1.0
    for dim, parts in pieces:
        steps = jax.random.uniform(jax.random.fold_in(jax.random.fold_in(own_key, 6), dim), (parts,), jnp.float32, low / len(pieces), largest / len(pieces))
        gain = gain * jnp.repeat(jnp.exp(steps), shape[dim] // parts).reshape((-1,) + (1,) * (len(shape) - 1 - dim))
    return gain


def noise(own_key, dims, scale, bound, cuts=(), kind=jnp.bfloat16):
    values = jax.random.normal(own_key, dims, jnp.float32) * scale
    if len(cuts) > 0:
        values = levels(own_key, dims, cuts, -0.22, 0.18) * values
    return jnp.clip(values, min=-bound, max=bound).astype(kind)


def setup_inputs(seed: int = 0) -> dict:
    arg_keys = jax.random.split(jax.random.key(seed), 9)
    tokens = noise(arg_keys[0], (TOKENS, D), 1.0, 6.0, ((0, 32),))
    expert_ids = draw_expert_ids(jax.random.fold_in(arg_keys[8], 71), 0)
    slot_ids = draw_slot_ids(jax.random.fold_in(arg_keys[8], 71), 0)
    dropped = draw_dropped(jax.random.fold_in(arg_keys[8], 71), 0)
    gates = jnp.clip(0.1 + 0.9 * jax.random.uniform(arg_keys[4], (TOKENS, 2), jnp.float32) ** levels(arg_keys[4], (TOKENS, 2), ((0, 32),), -0.2, 0.2), 0.1, 1.0)
    w_in = noise(arg_keys[5], (EXPERTS, D, FF), D ** -0.5, 0.15625, ((0, 4), (2, 8)))
    w_out = noise(arg_keys[6], (EXPERTS, FF, D), FF ** -0.5, 0.0625, ((0, 4), (1, 8)))
    out_grad = noise(arg_keys[7], (TOKENS, D), 1.0, 6.0, ((0, 32),))
    return {"tokens": tokens, "expert_ids": expert_ids, "slot_ids": slot_ids, "dropped": dropped, "gates": gates, "w_in": w_in, "w_out": w_out, "out_grad": out_grad}


inv_root_two = 0.7071067811865476
inv_root_two_pi = 0.3989422804014327


def gelu_exact(value):
    return 0.5 * value * (1.0 + lax.erf(value * inv_root_two))


def gelu_slope(value):
    return 0.5 * (1.0 + lax.erf(value * inv_root_two)) + value * jnp.exp(-0.5 * value * value) * inv_root_two_pi


def group_sum(left, right):
    count = left.shape[0]
    width = right.shape[1]
    group = FF // N_DP
    left_parts = left.reshape(count, N_DP, group).transpose(1, 0, 2)
    right_parts = right.reshape(N_DP, group, width)

    def add_group(total, pair):
        term = jnp.dot(pair[0], pair[1], preferred_element_type=jnp.float32).astype(jnp.bfloat16)
        return total + term.astype(jnp.float32), None

    total, unused = lax.scan(add_group, jnp.zeros((count, width), jnp.float32), (left_parts, right_parts))
    return total.astype(jnp.bfloat16)


def expert_pass(packed):
    rows, grad_rows, weight_in, weight_out = packed
    pre = jnp.dot(rows, weight_in, preferred_element_type=jnp.float32)
    hidden = gelu_exact(pre).astype(jnp.bfloat16)
    output = group_sum(hidden, weight_out)
    hidden_grad = jnp.dot(grad_rows, weight_out.T, preferred_element_type=jnp.float32)
    pre_grad = (hidden_grad * gelu_slope(pre)).astype(jnp.bfloat16)
    weight_out_grad = jnp.dot(hidden.T, grad_rows, preferred_element_type=jnp.float32)
    weight_in_grad = jnp.dot(rows.T, pre_grad, preferred_element_type=jnp.float32)
    row_grad = group_sum(pre_grad, weight_in.T)
    return output, row_grad, weight_in_grad, weight_out_grad


def reference(tokens, expert_ids, slot_ids, dropped, gates, w_in, w_out, out_grad):
    blocks = TOKENS // TOK_DEV
    columns = EXPERTS * CAP
    block_of = (jnp.arange(TOKENS, dtype=jnp.int32) // TOK_DEV).astype(jnp.int32)
    target = jnp.where(dropped == 0, expert_ids * CAP + slot_ids, columns).astype(jnp.int32)
    block_idx = jnp.broadcast_to(block_of[:, None], target.shape)
    token_rows = jnp.broadcast_to(tokens[:, None, :], (TOKENS, 2, D))
    buffer = jnp.zeros((blocks, columns + 1, D), jnp.bfloat16).at[block_idx, target].set(token_rows)
    scaled = (gates[:, :, None] * out_grad.astype(jnp.float32)[:, None, :]).astype(jnp.bfloat16)
    grad_buffer = jnp.zeros((blocks, columns + 1, D), jnp.bfloat16).at[block_idx, target].set(scaled)

    def by_expert(array):
        return array[:, :columns].reshape(blocks, EXPERTS, CAP, D).transpose(1, 0, 2, 3).reshape(EXPERTS, blocks * CAP, D)

    def by_block(array):
        back = array.reshape(EXPERTS, blocks, CAP, D).transpose(1, 0, 2, 3).reshape(blocks, columns, D)
        return jnp.concatenate([back, jnp.zeros((blocks, 1, D), back.dtype)], axis=1)

    outputs, row_grads, w_in_grad, w_out_grad = lax.map(expert_pass, (by_expert(buffer), by_expert(grad_buffer), w_in, w_out))
    picked = by_block(outputs)[block_idx, target].astype(jnp.float32)
    mixed = jnp.sum(gates[:, :, None] * picked, axis=1).astype(jnp.bfloat16)
    gate_grad = jnp.sum(picked * out_grad.astype(jnp.float32)[:, None, :], axis=-1)
    picked_grad = by_block(row_grads)[block_idx, target].astype(jnp.float32)
    tok_grad = jnp.sum(picked_grad, axis=1).astype(jnp.bfloat16)
    return mixed, tok_grad, gate_grad, w_in_grad, w_out_grad
```

```python
import functools

import jax
import jax.numpy as jnp
from jax import lax
from jax.experimental import pallas as pl
from jax.experimental.pallas import tpu as pltpu
from jax.sharding import Mesh
from jax.sharding import PartitionSpec as P

CAP = 4
CHUNK = 256
DONE = jax.ShapeDtypeStruct((8, 128), jnp.float32)


inv_root_two = 0.7071067811865476
inv_root_two_pi = 0.3989422804014327


def gelu_exact(value):
    return 0.5 * value * (1.0 + lax.erf(value * inv_root_two))


def gelu_slope(value):
    return (
        0.5 * (1.0 + lax.erf(value * inv_root_two))
        + value * jnp.exp(-0.5 * value * value) * inv_root_two_pi
    )


def contract(left, right, left_dim, right_dim):
    return lax.dot_general(
        left,
        right,
        (((left_dim,), (right_dim,)), ((), ())),
        preferred_element_type=jnp.float32,
    )


def order_matrix(expert, exp_local, count):
    shape = (count // exp_local, count)
    pick = lax.broadcasted_iota(jnp.int32, shape, 0)
    row = lax.broadcasted_iota(jnp.int32, shape, 1)
    wanted = (pick // CAP) * (CAP * exp_local) + expert * CAP + pick % CAP
    return (row == wanted).astype(jnp.bfloat16)


def slot_masks(ids_ref, slot_ref, dropped_ref, exp_local, columns):
    ids = ids_ref[...]
    group = jnp.bitwise_xor(ids // exp_local, lax.axis_index("expert"))
    target = (group * exp_local + ids % exp_local) * CAP + slot_ref[...]
    target = jnp.where(dropped_ref[...] == 0, target, -1)
    column = lax.broadcasted_iota(jnp.int32, (columns, target.shape[1]), 0)
    return [column == target[k : k + 1] for k in range(target.shape[0])]


def prepare_kernel(
    ids_ref, slot_ref, dropped_ref, gates_ref, tokens_ref, out_grad_ref, *outs, exp_local
):
    half = exp_local * CAP
    masks = slot_masks(ids_ref, slot_ref, dropped_ref, exp_local, half * len(outs))
    select = sum(mask.astype(jnp.float32) for mask in masks).astype(jnp.bfloat16)
    gate = sum(
        jnp.sum(jnp.where(mask, gates_ref[k : k + 1], 0.0), axis=1, keepdims=True)
        for k, mask in enumerate(masks)
    )
    rows = contract(select, tokens_ref[...], 1, 0)
    grads = contract(select, out_grad_ref[...], 1, 0) * gate
    for group, out_ref in enumerate(outs):
        part = slice(group * half, (group + 1) * half)
        out_ref[...] = jnp.concatenate([rows[part], grads[part]], axis=0).astype(jnp.bfloat16)


def stack_halves(refs):
    half = refs[0].shape[0] // 2
    wide = [ref[...].astype(jnp.float32) for ref in refs]
    return [
        jnp.concatenate([part[at : at + half] for part in wide], axis=0) for at in (0, half)
    ]


def finish_kernel(
    ids_ref, slot_ref, dropped_ref, gates_ref, out_grad_ref, *refs, exp_local
):
    parts, (mixed_ref, tok_grad_ref, gate_grad_ref) = refs[:-3], refs[-3:]
    returned, returned_grad = [rows.astype(jnp.bfloat16) for rows in stack_halves(parts)]
    masks = slot_masks(ids_ref, slot_ref, dropped_ref, exp_local, returned.shape[0])
    select = sum(mask.astype(jnp.float32) for mask in masks).astype(jnp.bfloat16)
    tok_grad_ref[...] = contract(select, returned_grad, 0, 0).astype(jnp.bfloat16)
    tokens = gates_ref.shape[1]
    gates = jnp.concatenate([gates_ref[...], jnp.zeros((6, tokens), jnp.float32)], axis=0).T
    wide = out_grad_ref[...].astype(jnp.float32)
    mixed = jnp.zeros(wide.shape, jnp.float32)
    grads = []
    for k, mask in enumerate(masks):
        picked = contract(mask.astype(jnp.bfloat16), returned, 0, 0)
        mixed = mixed + gates[:, k : k + 1] * picked
        grads.append(jnp.sum(picked * wide, axis=1, keepdims=True))
    mixed_ref[...] = mixed.astype(jnp.bfloat16)
    grads.append(jnp.zeros((tokens, 6), jnp.float32))
    gate_grad_ref[...] = jnp.concatenate(grads, axis=1).T[:2]


def split_kernel(after_ref, *refs):
    for out_ref, rows in zip(refs[-2:], stack_halves(refs[:-2])):
        out_ref[...] = rows.astype(jnp.bfloat16)


def pair_kernel(*refs):
    own_ref, mate_ref, out_ref = refs[-3:]
    half = own_ref.shape[0]
    out_ref[:half] = own_ref[...]
    out_ref[half:] = mate_ref[...]


def pass_kernel(*refs):
    refs[-1][...] = refs[-2][...]


def add(left_ref, right_ref):
    total = left_ref[...].astype(jnp.float32) + right_ref[...].astype(jnp.float32)
    return total.astype(jnp.bfloat16)


def add_kernel(*refs):
    left_ref, right_ref = refs[-3:-1]
    refs[-1][...] = add(left_ref, right_ref)


def add_split_kernel(*refs):
    left_ref, right_ref, mine_ref, other_ref = refs[-4:]
    half = mine_ref.shape[0]
    total = add(left_ref, right_ref)
    mine_ref[...] = total[:half]
    other_ref[...] = total[half:]


def join_kernel(*refs, groups):
    first_a, first_b, second_a, second_b = refs[-groups - 4 : -groups]
    first = add(first_a, first_b).astype(jnp.float32)
    second = add(second_a, second_b).astype(jnp.float32)
    half = first.shape[0] // groups
    for group, out_ref in enumerate(refs[-groups:]):
        part = slice(group * half, (group + 1) * half)
        out_ref[...] = jnp.concatenate([first[part], second[part]], axis=0).astype(jnp.bfloat16)


def hold_kernel(*refs):
    weight_ref, held_ref, done_ref, sems = refs[-4:]
    copies = [
        pltpu.make_async_copy(weight_ref.at[x], held_ref.at[x], sems.at[x])
        for x in range(weight_ref.shape[0])
    ]
    for copy in copies:
        copy.start()
    done_ref[...] = jnp.zeros(done_ref.shape, done_ref.dtype)
    for copy in copies:
        copy.wait()


def w_out_grad_kernel(*refs, skip, expert, at, chunk):
    hidden_ref, rows_ref = refs[skip : skip + 2]
    out_ref, done_ref, made, sems = refs[-4:]
    done_ref[...] = jnp.zeros(done_ref.shape, done_ref.dtype)
    copies = []
    for i, begin in enumerate(range(0, made.shape[0], chunk)):
        here, there = pl.ds(begin, chunk), pl.ds(at + begin, chunk)
        made[here] = contract(hidden_ref[expert, :, there], rows_ref[expert], 0, 0)
        copies.append(
            pltpu.make_async_copy(made.at[here], out_ref.at[expert, there], sems.at[i])
        )
        copies[-1].start()
    for copy in copies:
        copy.wait()


def w_in_grad_kernel(*refs, skip, expert, at, chunk):
    pre_grad_ref, rows_ref = refs[skip : skip + 2]
    out_ref, done_ref, made, sems = refs[-4:]
    done_ref[...] = jnp.zeros(done_ref.shape, done_ref.dtype)
    turned = rows_ref[expert].T
    copies = []
    for i, begin in enumerate(range(0, made.shape[1], chunk)):
        here, there = pl.ds(begin, chunk), pl.ds(at + begin, chunk)
        made[:, here] = contract(turned, pre_grad_ref[expert, :, there], 1, 0)
        copies.append(
            pltpu.make_async_copy(made.at[:, here], out_ref.at[expert, :, there], sems.at[i])
        )
        copies[-1].start()
    for copy in copies:
        copy.wait()


def params(rows):
    return pltpu.CompilerParams(vmem_limit_bytes=(6 << 20) + rows * (24 << 10))


def prepare(choices, gates, tokens, out_grad, groups, exp_local):
    block = (2 * exp_local * CAP, tokens.shape[1])
    whole = pl.BlockSpec(memory_space=pltpu.VMEM)
    return pl.pallas_call(
        functools.partial(prepare_kernel, exp_local=exp_local),
        out_specs=[whole] * groups,
        out_shape=[pltpu.VMEM(block, jnp.bfloat16)]
        + [jax.ShapeDtypeStruct(block, jnp.bfloat16)] * (groups - 1),
        compiler_params=pltpu.CompilerParams(vmem_limit_bytes=60 << 20),
        name="prepare",
    )(*choices, gates, tokens, out_grad)


def finish(choices, gates, out_grad, parts, exp_local):
    return pl.pallas_call(
        functools.partial(finish_kernel, exp_local=exp_local),
        out_shape=[
            jax.ShapeDtypeStruct(out_grad.shape, jnp.bfloat16),
            jax.ShapeDtypeStruct(out_grad.shape, jnp.bfloat16),
            jax.ShapeDtypeStruct(gates.shape, jnp.float32),
        ],
        compiler_params=params(out_grad.shape[0]),
        name="finish",
    )(*choices, gates, out_grad, *parts)


def small_call(kernel, name, after, operands, counts):
    width = operands[0].shape[1]
    results = pl.pallas_call(
        kernel,
        in_specs=[pl.BlockSpec(memory_space=pl.ANY)] * len(after)
        + [pl.BlockSpec(memory_space=pltpu.VMEM)] * len(operands),
        out_shape=[jax.ShapeDtypeStruct((count, width), jnp.bfloat16) for count in counts],
        compiler_params=params(4 * counts[0]),
        cost_estimate=order_cost(counts[0], width),
        name=name,
    )(*after, *operands)
    return list(results)


def hold(after, weight):
    return pl.pallas_call(
        hold_kernel,
        in_specs=[pl.BlockSpec(memory_space=pl.ANY)] * (len(after) + 1),
        out_specs=[pl.BlockSpec(memory_space=pltpu.VMEM)] * 2,
        out_shape=[pltpu.VMEM(weight.shape, weight.dtype), DONE],
        scratch_shapes=[pltpu.SemaphoreType.DMA((weight.shape[0],))],
        compiler_params=pltpu.CompilerParams(vmem_limit_bytes=42 << 20),
        cost_estimate=pl.CostEstimate(
            flops=0, bytes_accessed=4 * weight.size, transcendentals=0
        ),
        name="hold",
    )(*after, weight)


def weight_gradient(kernel, hidden, rows, shape, after, name, expert, part, parts, base=None):
    whole = pl.BlockSpec(memory_space=pltpu.VMEM)
    anywhere = pl.BlockSpec(memory_space=pl.ANY)
    width, units = rows.shape[2], hidden.shape[2] // parts
    chunk = min(CHUNK, units)
    made = (units, width) if kernel is w_out_grad_kernel else (width, units)
    operands = (*after, hidden, rows) + (() if base is None else (base,))
    return pl.pallas_call(
        functools.partial(kernel, skip=len(after), expert=expert, at=part * units, chunk=chunk),
        in_specs=[anywhere] * len(after) + [whole] * 2 + [anywhere] * (base is not None),
        out_specs=[anywhere, whole],
        out_shape=[jax.ShapeDtypeStruct(shape, jnp.float32), DONE],
        input_output_aliases={} if base is None else {len(operands) - 1: 0},
        scratch_shapes=[
            pltpu.VMEM(made, jnp.float32),
            pltpu.SemaphoreType.DMA((units // chunk,)),
        ],
        compiler_params=pltpu.CompilerParams(vmem_limit_bytes=24 << 20),
        cost_estimate=pl.CostEstimate(
            flops=2 * rows.shape[1] * units * width,
            bytes_accessed=4 * units * width,
            transcendentals=0,
        ),
        name=name,
    )(*operands)


def sort_kernel(after_ref, *refs, places):
    blocks, out_ref = refs[:-1], refs[-1]
    experts = out_ref.shape[0]
    count = blocks[0].shape[0]
    part = count // experts // 2
    for expert in range(experts):
        order = order_matrix(expert, experts, count)
        for step, ref in enumerate(blocks):
            rows = contract(order, ref[...], 1, 0).astype(jnp.bfloat16)
            for i in range(2):
                at = places[2 * step + i] * part
                out_ref[expert, at : at + part] = rows[i * part : (i + 1) * part]


def unsort_kernel(in_ref, *blocks, places):
    experts = in_ref.shape[0]
    count = blocks[0].shape[0]
    part = count // experts // 2
    order = jnp.concatenate(
        [order_matrix(expert, experts, count) for expert in range(experts)], axis=0
    )
    for step, ref in enumerate(blocks):
        piece = jnp.concatenate(
            [
                in_ref[expert, at * part : (at + 1) * part]
                for expert in range(experts)
                for at in places[2 * step : 2 * step + 2]
            ],
            axis=0,
        )
        ref[...] = contract(order, piece, 0, 0).astype(jnp.bfloat16)


def order_cost(count, width):
    return pl.CostEstimate(
        flops=2 * count * count * width, bytes_accessed=4 * count * width, transcendentals=0
    )


def sort_rows(blocks, experts, places, after):
    count, width = blocks[0].shape
    rows = len(blocks) * count // experts
    return pl.pallas_call(
        functools.partial(sort_kernel, places=places),
        in_specs=[pl.BlockSpec(memory_space=pl.ANY)]
        + [pl.BlockSpec(memory_space=pltpu.VMEM)] * len(blocks),
        out_shape=jax.ShapeDtypeStruct((experts, rows, width), jnp.bfloat16),
        compiler_params=params(rows),
        cost_estimate=order_cost(experts * rows, width),
        name="sort_rows",
    )(after, *blocks)


def unsort_rows(rows, places):
    experts, count, width = rows.shape
    steps = len(places) // 2
    block = experts * count // steps
    return pl.pallas_call(
        functools.partial(unsort_kernel, places=places),
        out_shape=[jax.ShapeDtypeStruct((block, width), jnp.bfloat16)] * steps,
        compiler_params=params(count),
        cost_estimate=order_cost(experts * count, width),
        name="unsort_rows",
    )(rows)


DP = ("far", "near", "pair")


def ring_mate(position, count, odd):
    if (position % 2 == 1) == odd:
        return (position + 1) % count
    return (position - 1) % count


def odd_edges(count):
    columns = count // 2
    ring = [2 * c for c in range(columns)] + [2 * c + 1 for c in reversed(range(columns))]
    return [(ring[i], ring[ring_mate(i, count, True)]) for i in range(count)]


def ring_order(count, odd):
    held = [[i, ring_mate(i, count, odd)] for i in range(count)]
    blocks = [list(pair) for pair in held]
    for _ in range(count // 2 - 1):
        odd = not odd
        held = [held[ring_mate(i, count, odd)] for i in range(count)]
        for mine, more in zip(blocks, held):
            mine += more
    return blocks


def regroup(count):
    even, odd = ring_order(count, False), ring_order(count, True)
    places = {tuple(e.index(block) for block in o) for e, o in zip(even, odd)}
    (place,) = places
    return place


def swap(block, odd):
    if odd:
        return lax.ppermute(block, DP, odd_edges(lax.axis_size(DP)))
    return lax.ppermute(block, "near", [(0, 1), (1, 0)])


def expert_swap(blocks):
    size = lax.axis_size("expert")
    got = [
        lax.ppermute(blocks[k], "expert", [(i, i ^ k) for i in range(size)])
        for k in reversed(range(1, size))
    ]
    return [blocks[0]] + got[::-1]


def per_device(tokens, expert_ids, slot_ids, dropped, gates, w_in, w_out, out_grad):
    n_expert = lax.axis_size("expert")
    n_dp = lax.axis_size(DP)
    steps = n_dp // 2
    exp_local = w_in.shape[0]
    count = n_expert * exp_local * CAP
    choices = (expert_ids.T, slot_ids.T, dropped.T)
    gates = gates.T
    send = prepare(choices, gates, tokens, out_grad, n_expert, exp_local)
    got = expert_swap(send)
    held_in, done_in = hold([], w_in)
    own_rows, own_grads = small_call(split_kernel, "split", [done_in], got, [count] * 2)

    mate_rows, mate_grads = swap(own_rows, False), swap(own_grads, True)
    pairs = [own_rows, mate_rows]
    row_blocks = small_call(pair_kernel, "pair", [mate_grads], pairs, [2 * count])
    pairs = [own_grads, mate_grads]
    grad_blocks = small_call(pair_kernel, "pair", [], pairs, [2 * count])
    held_out, done_out = hold([row_blocks[0], grad_blocks[0]], w_out)
    for step in range(1, steps):
        arrived = swap(row_blocks[-1], step % 2 == 1)
        if step == 1:
            (arrived,) = small_call(pass_kernel, "pass", [done_out], [arrived], [2 * count])
        row_blocks.append(arrived)
        grad_blocks.append(swap(grad_blocks[-1], step % 2 == 0))
    straight, crossed = range(n_dp), regroup(n_dp)
    rows = sort_rows(row_blocks, exp_local, straight, done_in)
    pre = jnp.einsum("xmd,xdf->xmf", rows, held_in, preferred_element_type=jnp.float32)
    hidden = gelu_exact(pre).astype(jnp.bfloat16)
    grad_rows = sort_rows(grad_blocks, exp_local, crossed, rows)
    hidden_grad = jnp.einsum(
        "xmd,xfd->xmf", grad_rows, held_out, preferred_element_type=jnp.float32
    )
    pre_grad = (hidden_grad * gelu_slope(pre)).astype(jnp.bfloat16)
    row_grad = jnp.einsum(
        "xmf,xdf->xmd", pre_grad, held_in, preferred_element_type=jnp.float32
    )
    back_blocks = unsort_rows(row_grad.astype(jnp.bfloat16), straight)
    output = jnp.einsum("xmf,xfd->xmd", hidden, held_out, preferred_element_type=jnp.float32)
    out_blocks = unsort_rows(output.astype(jnp.bfloat16), crossed)

    parts = 2
    work = [
        (kernel, left, right, shape, expert, part)
        for kernel, left, right, shape in (
            (w_out_grad_kernel, hidden, grad_rows, w_out.shape),
            (w_in_grad_kernel, pre_grad, rows, w_in.shape),
        )
        for expert in range(exp_local)
        for part in range(parts)
    ]
    made = {}

    def next_piece(after):
        if len(work) == 0:
            return after
        kernel, left, right, shape, expert, part = work.pop(0)
        name = kernel.__name__
        made[name], ready = weight_gradient(
            kernel, left, right, shape, [after], name, expert, part, parts, made.get(name)
        )
        return ready

    def add_step(after, block, arrived, step):
        if step > 1:
            return small_call(add_kernel, "add", after, [block, arrived], [2 * count])
        return small_call(add_split_kernel, "add_split", after, [block, arrived], [count] * 2)

    back_sum, out_sum = back_blocks[-1:], out_blocks[-1:]
    back_arrived, out_arrived = swap(back_sum[0], True), swap(out_sum[0], False)
    for step in range(steps - 1, 0, -1):
        ready = next_piece(out_sum[-1])
        back_sum = add_step([ready], back_blocks[step - 1], back_arrived, step)
        back_arrived = swap(back_sum[-1], step % 2 == 0)
        if step > 1:
            ready = next_piece(back_sum[-1])
        out_sum = add_step([ready], out_blocks[step - 1], out_arrived, step)
        out_arrived = swap(out_sum[-1], step % 2 == 1)
    joined = small_call(
        functools.partial(join_kernel, groups=n_expert),
        "join",
        [next_piece(out_sum[-1])],
        [out_sum[0], out_arrived, back_sum[0], back_arrived],
        [2 * exp_local * CAP] * n_expert,
    )
    while work:
        next_piece(joined[0])
    mixed, tok_grad, gate_grad = finish(
        choices, gates, out_grad, expert_swap(joined), exp_local
    )
    return (mixed, tok_grad, gate_grad.T, made["w_in_grad_kernel"], made["w_out_grad_kernel"])


def solution(mesh):
    n_expert, n_dp = mesh.shape["expert"], mesh.shape["dp"]
    split = Mesh(mesh.devices.reshape(n_expert, n_dp // 4, 2, 2), ("expert",) + DP)
    rows = P(("expert",) + DP, None)
    into = P("expert", None, DP)
    out_of = P("expert", DP, None)
    return jax.shard_map(
        per_device,
        mesh=split,
        in_specs=(rows, rows, rows, rows, rows, into, out_of, rows),
        out_specs=(rows, rows, rows, into, out_of),
        check_vma=False,
    )
```

```python
import functools

import jax
import jax.numpy as jnp
from jax import lax
from jax.experimental import pallas as pl
from jax.experimental.pallas import tpu as pltpu
from jax.sharding import Mesh
from jax.sharding import PartitionSpec as P

CAP = 4
CHUNK = 256
DONE = jax.ShapeDtypeStruct((8, 128), jnp.float32)


inv_root_two = 0.7071067811865476
inv_root_two_pi = 0.3989422804014327


def gelu_exact(value):
    return 0.5 * value * (1.0 + lax.erf(value * inv_root_two))


def gelu_slope(value):
    return (
        0.5 * (1.0 + lax.erf(value * inv_root_two))
        + value * jnp.exp(-0.5 * value * value) * inv_root_two_pi
    )


def contract(left, right, left_dim, right_dim):
    return lax.dot_general(
        left,
        right,
        (((left_dim,), (right_dim,)), ((), ())),
        preferred_element_type=jnp.float32,
    )


def order_matrix(count, exp_local):
    pick = lax.broadcasted_iota(jnp.int32, (count, count), 0)
    row = lax.broadcasted_iota(jnp.int32, (count, count), 1)
    kinds = 2 * exp_local
    each = count // kinds
    kind, rest = pick // each, pick % each
    wanted = (rest // CAP) * (CAP * kinds) + kind * CAP + rest % CAP
    return (row == wanted).astype(jnp.bfloat16)


def slot_masks(ids_ref, slot_ref, dropped_ref, exp_local, columns):
    ids = ids_ref[...]
    group = jnp.bitwise_xor(ids // exp_local, lax.axis_index("expert"))
    target = (group * exp_local + ids % exp_local) * CAP + slot_ref[...]
    target = jnp.where(dropped_ref[...] == 0, target, -1)
    column = lax.broadcasted_iota(jnp.int32, (columns, target.shape[1]), 0)
    return [column == target[k : k + 1] for k in range(target.shape[0])]


def prepare_kernel(
    ids_ref, slot_ref, dropped_ref, gates_ref, tokens_ref, out_grad_ref, *outs, exp_local
):
    half = exp_local * CAP
    masks = slot_masks(ids_ref, slot_ref, dropped_ref, exp_local, half * len(outs))
    select = sum(mask.astype(jnp.float32) for mask in masks).astype(jnp.bfloat16)
    gate = sum(
        jnp.sum(jnp.where(mask, gates_ref[k : k + 1], 0.0), axis=1, keepdims=True)
        for k, mask in enumerate(masks)
    )
    rows = contract(select, tokens_ref[...], 1, 0)
    grads = contract(select, out_grad_ref[...], 1, 0) * gate
    for group, out_ref in enumerate(outs):
        part = slice(group * half, (group + 1) * half)
        out_ref[...] = jnp.concatenate([rows[part], grads[part]], axis=0).astype(jnp.bfloat16)


def stack_halves(refs):
    half = refs[0].shape[0] // 2
    wide = [ref[...].astype(jnp.float32) for ref in refs]
    return [
        jnp.concatenate([part[at : at + half] for part in wide], axis=0) for at in (0, half)
    ]


def finish_kernel(
    ids_ref, slot_ref, dropped_ref, gates_ref, out_grad_ref, *refs, exp_local
):
    parts, (mixed_ref, tok_grad_ref, gate_grad_ref) = refs[:-3], refs[-3:]
    returned, returned_grad = [rows.astype(jnp.bfloat16) for rows in stack_halves(parts)]
    masks = slot_masks(ids_ref, slot_ref, dropped_ref, exp_local, returned.shape[0])
    select = sum(mask.astype(jnp.float32) for mask in masks).astype(jnp.bfloat16)
    tok_grad_ref[...] = contract(select, returned_grad, 0, 0).astype(jnp.bfloat16)
    tokens = gates_ref.shape[1]
    gates = jnp.concatenate([gates_ref[...], jnp.zeros((6, tokens), jnp.float32)], axis=0).T
    wide = out_grad_ref[...].astype(jnp.float32)
    mixed = jnp.zeros(wide.shape, jnp.float32)
    grads = []
    for k, mask in enumerate(masks):
        picked = contract(mask.astype(jnp.bfloat16), returned, 0, 0)
        mixed = mixed + gates[:, k : k + 1] * picked
        grads.append(jnp.sum(picked * wide, axis=1, keepdims=True))
    mixed_ref[...] = mixed.astype(jnp.bfloat16)
    grads.append(jnp.zeros((tokens, 6), jnp.float32))
    gate_grad_ref[...] = jnp.concatenate(grads, axis=1).T[:2]


def stack_kernel(*refs, skip):
    out_ref = refs[-1]
    for i, ref in enumerate(refs[skip:-1]):
        count = ref.shape[0]
        out_ref[i * count : (i + 1) * count] = ref[...]


def pass_kernel(*refs):
    refs[-1][...] = refs[-2][...]


def add(left_ref, right_ref):
    total = left_ref[...].astype(jnp.float32) + right_ref[...].astype(jnp.float32)
    return total.astype(jnp.bfloat16)


def add_kernel(*refs):
    left_ref, right_ref = refs[-3:-1]
    refs[-1][...] = add(left_ref, right_ref)


def add_split_kernel(*refs):
    left_ref, right_ref, mine_ref, other_ref = refs[-4:]
    half = mine_ref.shape[0]
    total = add(left_ref, right_ref)
    mine_ref[...] = total[:half]
    other_ref[...] = total[half:]


def join_kernel(left_ref, right_ref, *outs):
    total = add(left_ref, right_ref)
    for i, out_ref in enumerate(outs):
        count = out_ref.shape[0]
        out_ref[...] = total[i * count : (i + 1) * count]


def hold_kernel(*refs):
    weight_ref, held_ref, done_ref, sems = refs[-4:]
    copies = [
        pltpu.make_async_copy(weight_ref.at[x], held_ref.at[x], sems.at[x])
        for x in range(weight_ref.shape[0])
    ]
    for copy in copies:
        copy.start()
    done_ref[...] = jnp.zeros(done_ref.shape, done_ref.dtype)
    for copy in copies:
        copy.wait()


def w_out_grad_kernel(*refs, skip, expert, at, chunk):
    hidden_ref, rows_ref = refs[skip : skip + 2]
    out_ref, done_ref, made, sems = refs[-4:]
    done_ref[...] = jnp.zeros(done_ref.shape, done_ref.dtype)
    copies = []
    for i, begin in enumerate(range(0, made.shape[0], chunk)):
        here, there = pl.ds(begin, chunk), pl.ds(at + begin, chunk)
        made[here] = contract(hidden_ref[expert, :, there], rows_ref[expert], 0, 0)
        copies.append(
            pltpu.make_async_copy(made.at[here], out_ref.at[expert, there], sems.at[i])
        )
        copies[-1].start()
    for copy in copies:
        copy.wait()


def w_in_grad_kernel(*refs, skip, expert, at, chunk):
    pre_grad_ref, rows_ref = refs[skip : skip + 2]
    out_ref, done_ref, made, sems = refs[-4:]
    done_ref[...] = jnp.zeros(done_ref.shape, done_ref.dtype)
    turned = rows_ref[expert].T
    copies = []
    for i, begin in enumerate(range(0, made.shape[1], chunk)):
        here, there = pl.ds(begin, chunk), pl.ds(at + begin, chunk)
        made[:, here] = contract(turned, pre_grad_ref[expert, :, there], 1, 0)
        copies.append(
            pltpu.make_async_copy(made.at[:, here], out_ref.at[expert, :, there], sems.at[i])
        )
        copies[-1].start()
    for copy in copies:
        copy.wait()


def params(rows):
    return pltpu.CompilerParams(vmem_limit_bytes=(6 << 20) + rows * (24 << 10))


def prepare(choices, gates, tokens, out_grad, groups, exp_local):
    block = (2 * exp_local * CAP, tokens.shape[1])
    whole = pl.BlockSpec(memory_space=pltpu.VMEM)
    return pl.pallas_call(
        functools.partial(prepare_kernel, exp_local=exp_local),
        out_specs=[whole] * groups,
        out_shape=[pltpu.VMEM(block, jnp.bfloat16)]
        + [jax.ShapeDtypeStruct(block, jnp.bfloat16)] * (groups - 1),
        compiler_params=pltpu.CompilerParams(vmem_limit_bytes=60 << 20),
        name="prepare",
    )(*choices, gates, tokens, out_grad)


def finish(choices, gates, out_grad, parts, exp_local):
    return pl.pallas_call(
        functools.partial(finish_kernel, exp_local=exp_local),
        out_shape=[
            jax.ShapeDtypeStruct(out_grad.shape, jnp.bfloat16),
            jax.ShapeDtypeStruct(out_grad.shape, jnp.bfloat16),
            jax.ShapeDtypeStruct(gates.shape, jnp.float32),
        ],
        compiler_params=params(out_grad.shape[0]),
        name="finish",
    )(*choices, gates, out_grad, *parts)


def small_call(kernel, name, after, operands, counts):
    width = operands[0].shape[1]
    results = pl.pallas_call(
        kernel,
        in_specs=[pl.BlockSpec(memory_space=pl.ANY)] * len(after)
        + [pl.BlockSpec(memory_space=pltpu.VMEM)] * len(operands),
        out_shape=[jax.ShapeDtypeStruct((count, width), jnp.bfloat16) for count in counts],
        compiler_params=params(4 * counts[0]),
        cost_estimate=order_cost(counts[0], width),
        name=name,
    )(*after, *operands)
    return list(results)


def hold(after, weight):
    return pl.pallas_call(
        hold_kernel,
        in_specs=[pl.BlockSpec(memory_space=pl.ANY)] * (len(after) + 1),
        out_specs=[pl.BlockSpec(memory_space=pltpu.VMEM)] * 2,
        out_shape=[pltpu.VMEM(weight.shape, weight.dtype), DONE],
        scratch_shapes=[pltpu.SemaphoreType.DMA((weight.shape[0],))],
        compiler_params=pltpu.CompilerParams(vmem_limit_bytes=42 << 20),
        cost_estimate=pl.CostEstimate(
            flops=0, bytes_accessed=4 * weight.size, transcendentals=0
        ),
        name="hold",
    )(*after, weight)


def weight_gradient(kernel, hidden, rows, shape, after, name, expert, part, parts, base=None):
    whole = pl.BlockSpec(memory_space=pltpu.VMEM)
    anywhere = pl.BlockSpec(memory_space=pl.ANY)
    width, units = rows.shape[2], hidden.shape[2] // parts
    chunk = min(CHUNK, units)
    made = (units, width) if kernel is w_out_grad_kernel else (width, units)
    operands = (*after, hidden, rows) + (() if base is None else (base,))
    return pl.pallas_call(
        functools.partial(kernel, skip=len(after), expert=expert, at=part * units, chunk=chunk),
        in_specs=[anywhere] * len(after) + [whole] * 2 + [anywhere] * (base is not None),
        out_specs=[anywhere, whole],
        out_shape=[jax.ShapeDtypeStruct(shape, jnp.float32), DONE],
        input_output_aliases={} if base is None else {len(operands) - 1: 0},
        scratch_shapes=[
            pltpu.VMEM(made, jnp.float32),
            pltpu.SemaphoreType.DMA((units // chunk,)),
        ],
        compiler_params=pltpu.CompilerParams(vmem_limit_bytes=24 << 20),
        cost_estimate=pl.CostEstimate(
            flops=2 * rows.shape[1] * units * width,
            bytes_accessed=4 * units * width,
            transcendentals=0,
        ),
        name=name,
    )(*operands)


def sort_kernel(after_ref, *refs):
    blocks, outs = refs[:-2], refs[-2:]
    experts = outs[0].shape[0]
    count = blocks[0].shape[0] // 2
    part = count // (2 * experts)
    order = order_matrix(count, experts)
    for i in range(2 * len(blocks)):
        half = slice((i % 2) * count, (i % 2 + 1) * count)
        rows = contract(order, blocks[i // 2][half], 1, 0).astype(jnp.bfloat16)
        for kind in range(2 * experts):
            outs[kind // experts][kind % experts, i * part : (i + 1) * part] = rows[
                kind * part : (kind + 1) * part
            ]


def unsort_kernel(*refs):
    ins, blocks = refs[:2], refs[2:]
    experts = ins[0].shape[0]
    count = blocks[0].shape[0] // 2
    part = count // (2 * experts)
    order = order_matrix(count, experts)
    for i in range(2 * len(blocks)):
        at = slice(i * part, (i + 1) * part)
        piece = jnp.concatenate([ref[x, at] for ref in ins for x in range(experts)], axis=0)
        half = slice((i % 2) * count, (i % 2 + 1) * count)
        blocks[i // 2][half] = contract(order, piece, 0, 0).astype(jnp.bfloat16)


def order_cost(count, width):
    return pl.CostEstimate(
        flops=2 * count * count * width, bytes_accessed=4 * count * width, transcendentals=0
    )


def sort_rows(blocks, experts, after):
    count, width = blocks[0].shape
    rows = len(blocks) * count // (2 * experts)
    return pl.pallas_call(
        sort_kernel,
        in_specs=[pl.BlockSpec(memory_space=pl.ANY)]
        + [pl.BlockSpec(memory_space=pltpu.VMEM)] * len(blocks),
        out_shape=[jax.ShapeDtypeStruct((experts, rows, width), jnp.bfloat16)] * 2,
        compiler_params=params(2 * rows),
        cost_estimate=order_cost(2 * experts * rows, width),
        name="sort_rows",
    )(after, *blocks)


def unsort_rows(first, second, steps):
    experts, count, width = first.shape
    block = 2 * experts * count // steps
    return pl.pallas_call(
        unsort_kernel,
        out_shape=[jax.ShapeDtypeStruct((block, width), jnp.bfloat16)] * steps,
        compiler_params=params(2 * count),
        cost_estimate=order_cost(2 * experts * count, width),
        name="unsort_rows",
    )(first, second)


DP = ("far", "near", "pair")


def ring_mate(position, count, odd):
    if (position % 2 == 1) == odd:
        return (position + 1) % count
    return (position - 1) % count


def ring_edges(count, odd):
    columns = count // 2
    ring = [2 * c for c in range(columns)] + [2 * c + 1 for c in reversed(range(columns))]
    return [(ring[i], ring[ring_mate(i, count, odd)]) for i in range(count)]


def swap(block, phase):
    n_expert, n_dp = lax.axis_size("expert"), lax.axis_size(DP)
    pairs = [
        (e * n_dp + i, e * n_dp + j)
        for e in range(n_expert)
        for i, j in ring_edges(n_dp, (phase + e) % 2 == 1)
    ]
    return lax.ppermute(block, ("expert",) + DP, pairs)


def expert_swap(blocks):
    size = lax.axis_size("expert")
    got = [
        lax.ppermute(blocks[k], "expert", [(i, i ^ k) for i in range(size)])
        for k in reversed(range(1, size))
    ]
    return [blocks[0]] + got[::-1]


def per_device(tokens, expert_ids, slot_ids, dropped, gates, w_in, w_out, out_grad):
    n_expert = lax.axis_size("expert")
    n_dp = lax.axis_size(DP)
    steps = n_dp // 2
    exp_local = w_in.shape[0]
    count = 2 * n_expert * exp_local * CAP
    choices = (expert_ids.T, slot_ids.T, dropped.T)
    gates = gates.T
    send = prepare(choices, gates, tokens, out_grad, n_expert, exp_local)
    got = expert_swap(send)
    held_in, done_in = hold([], w_in)
    stack = functools.partial(stack_kernel, skip=1)
    (own,) = small_call(stack, "stack", [done_in], got, [count])

    stack = functools.partial(stack_kernel, skip=0)
    blocks = small_call(stack, "pair", [], [own, swap(own, 0)], [2 * count])
    held_out, done_out = hold(blocks, w_out)
    for step in range(1, steps):
        arrived = swap(blocks[-1], step)
        if step == 1:
            (arrived,) = small_call(pass_kernel, "pass", [done_out], [arrived], [2 * count])
        blocks.append(arrived)
    rows, grad_rows = sort_rows(blocks, exp_local, done_in)
    pre = jnp.einsum("xmd,xdf->xmf", rows, held_in, preferred_element_type=jnp.float32)
    hidden = gelu_exact(pre).astype(jnp.bfloat16)
    output = jnp.einsum("xmf,xfd->xmd", hidden, held_out, preferred_element_type=jnp.float32)
    hidden_grad = jnp.einsum(
        "xmd,xfd->xmf", grad_rows, held_out, preferred_element_type=jnp.float32
    )
    pre_grad = (hidden_grad * gelu_slope(pre)).astype(jnp.bfloat16)
    row_grad = jnp.einsum(
        "xmf,xdf->xmd", pre_grad, held_in, preferred_element_type=jnp.float32
    )
    blocks = unsort_rows(output.astype(jnp.bfloat16), row_grad.astype(jnp.bfloat16), steps)

    parts = 1
    work = [
        (kernel, left, right, shape, expert, part)
        for kernel, left, right, shape in (
            (w_out_grad_kernel, hidden, grad_rows, w_out.shape),
            (w_in_grad_kernel, pre_grad, rows, w_in.shape),
        )
        for expert in range(exp_local)
        for part in range(parts)
    ]
    made = {}

    def next_piece(after):
        if len(work) == 0:
            return after
        kernel, left, right, shape, expert, part = work.pop(0)
        name = kernel.__name__
        made[name], ready = weight_gradient(
            kernel, left, right, shape, [after], name, expert, part, parts, made.get(name)
        )
        return ready

    def add_step(after, block, arrived, step):
        if step > 1:
            return small_call(add_kernel, "add", after, [block, arrived], [2 * count])
        return small_call(add_split_kernel, "add_split", after, [block, arrived], [count] * 2)

    total = blocks[-1:]
    for step in range(steps - 1, 0, -1):
        arrived = swap(total[-1], step)
        ready = next_piece(total[-1]) if len(work) > 1 else total[-1]
        total = add_step([ready], blocks[step - 1], arrived, step)
    arrived = swap(total[-1], 0)
    joined = small_call(
        join_kernel, "join", [], [total[0], arrived], [2 * exp_local * CAP] * n_expert
    )
    while work:
        next_piece(joined[0])
    mixed, tok_grad, gate_grad = finish(
        choices, gates, out_grad, expert_swap(joined), exp_local
    )
    return (mixed, tok_grad, gate_grad.T, made["w_in_grad_kernel"], made["w_out_grad_kernel"])


def solution(mesh):
    n_expert, n_dp = mesh.shape["expert"], mesh.shape["dp"]
    split = Mesh(mesh.devices.reshape(n_expert, n_dp // 4, 2, 2), ("expert",) + DP)
    rows = P(("expert",) + DP, None)
    into = P("expert", None, DP)
    out_of = P("expert", DP, None)
    return jax.shard_map(
        per_device,
        mesh=split,
        in_specs=(rows, rows, rows, rows, rows, into, out_of, rows),
        out_specs=(rows, rows, rows, into, out_of),
        check_vma=False,
    )
```

```python
import functools

import jax
import jax.numpy as jnp
from jax import lax
from jax.experimental import pallas as pl
from jax.experimental.pallas import tpu as pltpu
from jax.sharding import Mesh
from jax.sharding import PartitionSpec as P

CAP = 4
CHUNK = 256
DONE = jax.ShapeDtypeStruct((8, 128), jnp.float32)


inv_root_two = 0.7071067811865476
inv_root_two_pi = 0.3989422804014327


def gelu_exact(value):
    return 0.5 * value * (1.0 + lax.erf(value * inv_root_two))


def gelu_slope(value):
    return (
        0.5 * (1.0 + lax.erf(value * inv_root_two))
        + value * jnp.exp(-0.5 * value * value) * inv_root_two_pi
    )


def contract(left, right, left_dim, right_dim):
    return lax.dot_general(
        left,
        right,
        (((left_dim,), (right_dim,)), ((), ())),
        preferred_element_type=jnp.float32,
    )


def order_matrix(expert, exp_local, count):
    shape = (count // exp_local, count)
    pick = lax.broadcasted_iota(jnp.int32, shape, 0)
    row = lax.broadcasted_iota(jnp.int32, shape, 1)
    wanted = (pick // CAP) * (CAP * exp_local) + expert * CAP + pick % CAP
    return (row == wanted).astype(jnp.bfloat16)


def slot_masks(ids_ref, slot_ref, dropped_ref, exp_local, columns):
    ids = ids_ref[...]
    group = jnp.bitwise_xor(ids // exp_local, lax.axis_index("expert"))
    target = (group * exp_local + ids % exp_local) * CAP + slot_ref[...]
    target = jnp.where(dropped_ref[...] == 0, target, -1)
    column = lax.broadcasted_iota(jnp.int32, (columns, target.shape[1]), 0)
    return [column == target[k : k + 1] for k in range(target.shape[0])]


def prepare_kernel(
    ids_ref, slot_ref, dropped_ref, gates_ref, tokens_ref, out_grad_ref, *outs, exp_local
):
    half = exp_local * CAP
    masks = slot_masks(ids_ref, slot_ref, dropped_ref, exp_local, half * len(outs))
    select = sum(mask.astype(jnp.float32) for mask in masks).astype(jnp.bfloat16)
    gate = sum(
        jnp.sum(jnp.where(mask, gates_ref[k : k + 1], 0.0), axis=1, keepdims=True)
        for k, mask in enumerate(masks)
    )
    rows = contract(select, tokens_ref[...], 1, 0)
    grads = contract(select, out_grad_ref[...], 1, 0) * gate
    for group, out_ref in enumerate(outs):
        part = slice(group * half, (group + 1) * half)
        out_ref[...] = jnp.concatenate([rows[part], grads[part]], axis=0).astype(jnp.bfloat16)


def stack_halves(refs):
    half = refs[0].shape[0] // 2
    wide = [ref[...].astype(jnp.float32) for ref in refs]
    return [
        jnp.concatenate([part[at : at + half] for part in wide], axis=0) for at in (0, half)
    ]


def finish_kernel(
    ids_ref, slot_ref, dropped_ref, gates_ref, out_grad_ref, *refs, exp_local
):
    parts, (mixed_ref, tok_grad_ref, gate_grad_ref) = refs[:-3], refs[-3:]
    returned, returned_grad = [rows.astype(jnp.bfloat16) for rows in stack_halves(parts)]
    masks = slot_masks(ids_ref, slot_ref, dropped_ref, exp_local, returned.shape[0])
    select = sum(mask.astype(jnp.float32) for mask in masks).astype(jnp.bfloat16)
    tok_grad_ref[...] = contract(select, returned_grad, 0, 0).astype(jnp.bfloat16)
    tokens = gates_ref.shape[1]
    gates = jnp.concatenate([gates_ref[...], jnp.zeros((6, tokens), jnp.float32)], axis=0).T
    wide = out_grad_ref[...].astype(jnp.float32)
    mixed = jnp.zeros(wide.shape, jnp.float32)
    grads = []
    for k, mask in enumerate(masks):
        picked = contract(mask.astype(jnp.bfloat16), returned, 0, 0)
        mixed = mixed + gates[:, k : k + 1] * picked
        grads.append(jnp.sum(picked * wide, axis=1, keepdims=True))
    mixed_ref[...] = mixed.astype(jnp.bfloat16)
    grads.append(jnp.zeros((tokens, 6), jnp.float32))
    gate_grad_ref[...] = jnp.concatenate(grads, axis=1).T[:2]


def split_kernel(after_ref, *refs):
    for out_ref, rows in zip(refs[-2:], stack_halves(refs[:-2])):
        out_ref[...] = rows.astype(jnp.bfloat16)


def pair_kernel(*refs):
    own_ref, mate_ref, out_ref = refs[-3:]
    half = own_ref.shape[0]
    out_ref[:half] = own_ref[...]
    out_ref[half:] = mate_ref[...]


def pass_kernel(*refs):
    refs[-1][...] = refs[-2][...]


def add(left_ref, right_ref):
    total = left_ref[...].astype(jnp.float32) + right_ref[...].astype(jnp.float32)
    return total.astype(jnp.bfloat16)


def add_kernel(*refs):
    left_ref, right_ref = refs[-3:-1]
    refs[-1][...] = add(left_ref, right_ref)


def add_split_kernel(*refs):
    left_ref, right_ref, mine_ref, other_ref = refs[-4:]
    half = mine_ref.shape[0]
    total = add(left_ref, right_ref)
    mine_ref[...] = total[:half]
    other_ref[...] = total[half:]


def join_kernel(*refs, groups):
    first_a, first_b, second_a, second_b = refs[-groups - 4 : -groups]
    first = add(first_a, first_b).astype(jnp.float32)
    second = add(second_a, second_b).astype(jnp.float32)
    half = first.shape[0] // groups
    for group, out_ref in enumerate(refs[-groups:]):
        part = slice(group * half, (group + 1) * half)
        out_ref[...] = jnp.concatenate([first[part], second[part]], axis=0).astype(jnp.bfloat16)


def hold_kernel(*refs):
    weight_ref, held_ref, done_ref, sems = refs[-4:]
    copies = [
        pltpu.make_async_copy(weight_ref.at[x], held_ref.at[x], sems.at[x])
        for x in range(weight_ref.shape[0])
    ]
    for copy in copies:
        copy.start()
    done_ref[...] = jnp.zeros(done_ref.shape, done_ref.dtype)
    for copy in copies:
        copy.wait()


def w_out_grad_kernel(*refs, skip, expert, at, chunk):
    hidden_ref, rows_ref = refs[skip : skip + 2]
    out_ref, done_ref, made, sems = refs[-4:]
    done_ref[...] = jnp.zeros(done_ref.shape, done_ref.dtype)
    copies = []
    for i, begin in enumerate(range(0, made.shape[0], chunk)):
        here, there = pl.ds(begin, chunk), pl.ds(at + begin, chunk)
        made[here] = contract(hidden_ref[expert, :, there], rows_ref[expert], 0, 0)
        copies.append(
            pltpu.make_async_copy(made.at[here], out_ref.at[expert, there], sems.at[i])
        )
        copies[-1].start()
    for copy in copies:
        copy.wait()


def w_in_grad_kernel(*refs, skip, expert, at, chunk):
    pre_grad_ref, rows_ref = refs[skip : skip + 2]
    out_ref, done_ref, made, sems = refs[-4:]
    done_ref[...] = jnp.zeros(done_ref.shape, done_ref.dtype)
    turned = rows_ref[expert].T
    copies = []
    for i, begin in enumerate(range(0, made.shape[1], chunk)):
        here, there = pl.ds(begin, chunk), pl.ds(at + begin, chunk)
        made[:, here] = contract(turned, pre_grad_ref[expert, :, there], 1, 0)
        copies.append(
            pltpu.make_async_copy(made.at[:, here], out_ref.at[expert, :, there], sems.at[i])
        )
        copies[-1].start()
    for copy in copies:
        copy.wait()


def params(rows):
    return pltpu.CompilerParams(vmem_limit_bytes=(6 << 20) + rows * (24 << 10))


def prepare(choices, gates, tokens, out_grad, groups, exp_local):
    block = (2 * exp_local * CAP, tokens.shape[1])
    whole = pl.BlockSpec(memory_space=pltpu.VMEM)
    return pl.pallas_call(
        functools.partial(prepare_kernel, exp_local=exp_local),
        out_specs=[whole] * groups,
        out_shape=[pltpu.VMEM(block, jnp.bfloat16)]
        + [jax.ShapeDtypeStruct(block, jnp.bfloat16)] * (groups - 1),
        compiler_params=pltpu.CompilerParams(vmem_limit_bytes=60 << 20),
        name="prepare",
    )(*choices, gates, tokens, out_grad)


def finish(choices, gates, out_grad, parts, exp_local):
    return pl.pallas_call(
        functools.partial(finish_kernel, exp_local=exp_local),
        out_shape=[
            jax.ShapeDtypeStruct(out_grad.shape, jnp.bfloat16),
            jax.ShapeDtypeStruct(out_grad.shape, jnp.bfloat16),
            jax.ShapeDtypeStruct(gates.shape, jnp.float32),
        ],
        compiler_params=params(out_grad.shape[0]),
        name="finish",
    )(*choices, gates, out_grad, *parts)


def small_call(kernel, name, after, operands, counts):
    width = operands[0].shape[1]
    results = pl.pallas_call(
        kernel,
        in_specs=[pl.BlockSpec(memory_space=pl.ANY)] * len(after)
        + [pl.BlockSpec(memory_space=pltpu.VMEM)] * len(operands),
        out_shape=[jax.ShapeDtypeStruct((count, width), jnp.bfloat16) for count in counts],
        compiler_params=params(4 * counts[0]),
        cost_estimate=order_cost(counts[0], width),
        name=name,
    )(*after, *operands)
    return list(results)


def hold(after, weight):
    return pl.pallas_call(
        hold_kernel,
        in_specs=[pl.BlockSpec(memory_space=pl.ANY)] * (len(after) + 1),
        out_specs=[pl.BlockSpec(memory_space=pltpu.VMEM)] * 2,
        out_shape=[pltpu.VMEM(weight.shape, weight.dtype), DONE],
        scratch_shapes=[pltpu.SemaphoreType.DMA((weight.shape[0],))],
        compiler_params=pltpu.CompilerParams(vmem_limit_bytes=42 << 20),
        cost_estimate=pl.CostEstimate(
            flops=0, bytes_accessed=4 * weight.size, transcendentals=0
        ),
        name="hold",
    )(*after, weight)


def weight_gradient(kernel, hidden, rows, shape, after, name, expert, part, parts, base=None):
    whole = pl.BlockSpec(memory_space=pltpu.VMEM)
    anywhere = pl.BlockSpec(memory_space=pl.ANY)
    width, units = rows.shape[2], hidden.shape[2] // parts
    chunk = min(CHUNK // 2 if kernel is w_out_grad_kernel else CHUNK, units)
    made = (units, width) if kernel is w_out_grad_kernel else (width, units)
    operands = (*after, hidden, rows) + (() if base is None else (base,))
    return pl.pallas_call(
        functools.partial(kernel, skip=len(after), expert=expert, at=part * units, chunk=chunk),
        in_specs=[anywhere] * len(after) + [whole] * 2 + [anywhere] * (base is not None),
        out_specs=[anywhere, whole],
        out_shape=[jax.ShapeDtypeStruct(shape, jnp.float32), DONE],
        input_output_aliases={} if base is None else {len(operands) - 1: 0},
        scratch_shapes=[
            pltpu.VMEM(made, jnp.float32),
            pltpu.SemaphoreType.DMA((units // chunk,)),
        ],
        compiler_params=pltpu.CompilerParams(vmem_limit_bytes=24 << 20),
        cost_estimate=pl.CostEstimate(
            flops=2 * rows.shape[1] * units * width,
            bytes_accessed=4 * units * width,
            transcendentals=0,
        ),
        name=name,
    )(*operands)


def sort_kernel(after_ref, *refs, places):
    blocks, out_ref = refs[:-1], refs[-1]
    experts = out_ref.shape[0]
    count = blocks[0].shape[0]
    part = count // experts // 2
    for expert in range(experts):
        order = order_matrix(expert, experts, count)
        for step, ref in enumerate(blocks):
            rows = contract(order, ref[...], 1, 0).astype(jnp.bfloat16)
            for i in range(2):
                at = places[2 * step + i] * part
                out_ref[expert, at : at + part] = rows[i * part : (i + 1) * part]


def unsort_kernel(after_ref, in_ref, *blocks):
    experts = in_ref.shape[0]
    count = blocks[0].shape[0]
    part = count // experts
    order = jnp.concatenate(
        [order_matrix(expert, experts, count) for expert in range(experts)], axis=0
    )
    for step, ref in enumerate(blocks):
        piece = jnp.concatenate(
            [in_ref[expert, step * part : (step + 1) * part] for expert in range(experts)], axis=0
        )
        ref[...] = contract(order, piece, 0, 0).astype(jnp.bfloat16)


def order_cost(count, width):
    return pl.CostEstimate(
        flops=2 * count * count * width, bytes_accessed=4 * count * width, transcendentals=0
    )


def sort_rows(blocks, experts, places, after):
    count, width = blocks[0].shape
    rows = len(blocks) * count // experts
    return pl.pallas_call(
        functools.partial(sort_kernel, places=places),
        in_specs=[pl.BlockSpec(memory_space=pl.ANY)]
        + [pl.BlockSpec(memory_space=pltpu.VMEM)] * len(blocks),
        out_shape=jax.ShapeDtypeStruct((experts, rows, width), jnp.bfloat16),
        compiler_params=params(rows),
        cost_estimate=order_cost(experts * rows, width),
        name="sort_rows",
    )(after, *blocks)


def unsort_rows(rows, steps, after):
    experts, count, width = rows.shape
    block = experts * count // steps
    return pl.pallas_call(
        unsort_kernel,
        in_specs=[pl.BlockSpec(memory_space=pl.ANY), pl.BlockSpec(memory_space=pltpu.VMEM)],
        out_shape=[jax.ShapeDtypeStruct((block, width), jnp.bfloat16)] * steps,
        compiler_params=params(count),
        cost_estimate=order_cost(experts * count, width),
        name="unsort_rows",
    )(after, rows)


DP = ("far", "near", "pair")


def ring_mate(position, count, odd):
    if (position % 2 == 1) == odd:
        return (position + 1) % count
    return (position - 1) % count


def odd_edges(count):
    columns = count // 2
    ring = [2 * c for c in range(columns)] + [2 * c + 1 for c in reversed(range(columns))]
    return [(ring[i], ring[ring_mate(i, count, True)]) for i in range(count)]


def ring_order(count, odd):
    held = [[i, ring_mate(i, count, odd)] for i in range(count)]
    blocks = [list(pair) for pair in held]
    for _ in range(count // 2 - 1):
        odd = not odd
        held = [held[ring_mate(i, count, odd)] for i in range(count)]
        for mine, more in zip(blocks, held):
            mine += more
    return blocks


def regroup(count):
    even, odd = ring_order(count, False), ring_order(count, True)
    places = {tuple(e.index(block) for block in o) for e, o in zip(even, odd)}
    (place,) = places
    return place


def swap(block, odd):
    if odd:
        return lax.ppermute(block, DP, odd_edges(lax.axis_size(DP)))
    return lax.ppermute(block, "near", [(0, 1), (1, 0)])


def expert_swap(blocks):
    size = lax.axis_size("expert")
    got = [
        lax.ppermute(blocks[k], "expert", [(i, i ^ k) for i in range(size)])
        for k in reversed(range(1, size))
    ]
    return [blocks[0]] + got[::-1]


def per_device(tokens, expert_ids, slot_ids, dropped, gates, w_in, w_out, out_grad):
    n_expert = lax.axis_size("expert")
    n_dp = lax.axis_size(DP)
    steps = n_dp // 2
    exp_local = w_in.shape[0]
    count = n_expert * exp_local * CAP
    choices = (expert_ids.T, slot_ids.T, dropped.T)
    gates = gates.T
    send = prepare(choices, gates, tokens, out_grad, n_expert, exp_local)
    got = expert_swap(send)
    held_in, done_in = hold([], w_in)
    own_rows, own_grads = small_call(split_kernel, "split", [done_in], got, [count] * 2)

    mate_rows, mate_grads = swap(own_rows, False), swap(own_grads, True)
    pairs = [own_rows, mate_rows]
    row_blocks = small_call(pair_kernel, "pair", [mate_grads], pairs, [2 * count])
    pairs = [own_grads, mate_grads]
    grad_blocks = small_call(pair_kernel, "pair", [], pairs, [2 * count])
    held_out, done_out = hold([row_blocks[0], grad_blocks[0]], w_out)
    for step in range(1, steps):
        arrived = swap(row_blocks[-1], step % 2 == 1)
        if step == 1:
            (arrived,) = small_call(pass_kernel, "pass", [done_out], [arrived], [2 * count])
        row_blocks.append(arrived)
        grad_blocks.append(swap(grad_blocks[-1], step % 2 == 0))
    rows = sort_rows(row_blocks, exp_local, range(n_dp), done_in)
    pre = jnp.einsum("xmd,xdf->xmf", rows, held_in, preferred_element_type=jnp.float32)
    hidden = gelu_exact(pre).astype(jnp.bfloat16)
    output = jnp.einsum("xmf,xfd->xmd", hidden, held_out, preferred_element_type=jnp.float32)
    out_blocks = unsort_rows(output.astype(jnp.bfloat16), steps, done_out)
    grad_rows = sort_rows(grad_blocks, exp_local, regroup(n_dp), out_blocks[-1])
    hidden_grad = jnp.einsum(
        "xmd,xfd->xmf", grad_rows, held_out, preferred_element_type=jnp.float32
    )
    pre_grad = (hidden_grad * gelu_slope(pre)).astype(jnp.bfloat16)
    row_grad = jnp.einsum(
        "xmf,xdf->xmd", pre_grad, held_in, preferred_element_type=jnp.float32
    )

    parts = 1
    work = [
        (kernel, left, right, shape, expert, part)
        for kernel, left, right, shape in (
            (w_out_grad_kernel, hidden, grad_rows, w_out.shape),
            (w_in_grad_kernel, pre_grad, rows, w_in.shape),
        )
        for expert in range(exp_local)
        for part in range(parts)
    ]
    made = {}

    def next_piece(after):
        if len(work) == 0:
            return after
        kernel, left, right, shape, expert, part = work.pop(0)
        name = kernel.__name__
        made[name], ready = weight_gradient(
            kernel, left, right, shape, [after], name, expert, part, parts, made.get(name)
        )
        return ready

    def add_step(after, block, arrived, step):
        if step > 1:
            return small_call(add_kernel, "add", after, [block, arrived], [2 * count])
        return small_call(add_split_kernel, "add_split", after, [block, arrived], [count] * 2)

    last = steps - 1
    out_sum = out_blocks[last:]
    out_arrived = swap(out_sum[0], last % 2 == 1)
    for step in range(last, 0, -1):
        if step < last:
            back_arrived = swap(back_sum[-1], step % 2 == 1)
        ready = [next_piece(back_sum[-1])] if step == 1 < last else []
        out_sum = add_step(ready, out_blocks[step - 1], out_arrived, step)
        out_arrived = swap(out_sum[-1], step % 2 == 0)
        if step == last:
            back_blocks = unsort_rows(row_grad.astype(jnp.bfloat16), steps, out_sum[0])
            back_sum = back_blocks[last:]
            back_arrived = swap(back_sum[-1], step % 2 == 1)
            ready = [next_piece(back_sum[-1])]
        back_sum = add_step(ready, back_blocks[step - 1], back_arrived, step)
    back_arrived = swap(back_sum[-1], False)
    joined = small_call(
        functools.partial(join_kernel, groups=n_expert),
        "join",
        [next_piece(back_sum[-1])],
        [out_sum[0], out_arrived, back_sum[0], back_arrived],
        [2 * exp_local * CAP] * n_expert,
    )
    while work:
        next_piece(joined[0])
    mixed, tok_grad, gate_grad = finish(
        choices, gates, out_grad, expert_swap(joined), exp_local
    )
    return (mixed, tok_grad, gate_grad.T, made["w_in_grad_kernel"], made["w_out_grad_kernel"])


def solution(mesh):
    n_expert, n_dp = mesh.shape["expert"], mesh.shape["dp"]
    split = Mesh(mesh.devices.reshape(n_expert, n_dp // 4, 2, 2), ("expert",) + DP)
    rows = P(("expert",) + DP, None)
    into = P("expert", None, DP)
    out_of = P("expert", DP, None)
    return jax.shard_map(
        per_device,
        mesh=split,
        in_specs=(rows, rows, rows, rows, rows, into, out_of, rows),
        out_specs=(rows, rows, rows, into, out_of),
        check_vma=False,
    )
```

```python
import functools

import jax
import jax.numpy as jnp
from jax import lax
from jax.experimental import pallas as pl
from jax.experimental.pallas import tpu as pltpu
from jax.sharding import Mesh
from jax.sharding import PartitionSpec as P

CAP = 4
CHUNK = 256
DONE = jax.ShapeDtypeStruct((8, 128), jnp.float32)


inv_root_two = 0.7071067811865476
inv_root_two_pi = 0.3989422804014327


def gelu_exact(value):
    return 0.5 * value * (1.0 + lax.erf(value * inv_root_two))


def gelu_slope(value):
    return (
        0.5 * (1.0 + lax.erf(value * inv_root_two))
        + value * jnp.exp(-0.5 * value * value) * inv_root_two_pi
    )


def contract(left, right, left_dim, right_dim):
    return lax.dot_general(
        left,
        right,
        (((left_dim,), (right_dim,)), ((), ())),
        preferred_element_type=jnp.float32,
    )


def order_matrix(exp_local, count):
    pick = lax.broadcasted_iota(jnp.int32, (count, count), 0)
    row = lax.broadcasted_iota(jnp.int32, (count, count), 1)
    each = count // exp_local
    expert, rest = pick // each, pick % each
    wanted = (rest // CAP) * (CAP * exp_local) + expert * CAP + rest % CAP
    return (row == wanted).astype(jnp.bfloat16)


def slot_masks(ids_ref, slot_ref, dropped_ref, exp_local, columns):
    ids = ids_ref[...]
    group = jnp.bitwise_xor(ids // exp_local, lax.axis_index("expert"))
    target = (group * exp_local + ids % exp_local) * CAP + slot_ref[...]
    target = jnp.where(dropped_ref[...] == 0, target, -1)
    column = lax.broadcasted_iota(jnp.int32, (columns, target.shape[1]), 0)
    return [column == target[k : k + 1] for k in range(target.shape[0])]


def prepare_kernel(
    ids_ref, slot_ref, dropped_ref, gates_ref, tokens_ref, out_grad_ref, *outs, exp_local
):
    half = exp_local * CAP
    masks = slot_masks(ids_ref, slot_ref, dropped_ref, exp_local, half * len(outs))
    select = sum(mask.astype(jnp.float32) for mask in masks).astype(jnp.bfloat16)
    gate = sum(
        jnp.sum(jnp.where(mask, gates_ref[k : k + 1], 0.0), axis=1, keepdims=True)
        for k, mask in enumerate(masks)
    )
    rows = contract(select, tokens_ref[...], 1, 0)
    grads = contract(select, out_grad_ref[...], 1, 0) * gate
    for group, out_ref in enumerate(outs):
        part = slice(group * half, (group + 1) * half)
        out_ref[...] = jnp.concatenate([rows[part], grads[part]], axis=0).astype(jnp.bfloat16)


def stack_halves(refs):
    half = refs[0].shape[0] // 2
    wide = [ref[...].astype(jnp.float32) for ref in refs]
    return [
        jnp.concatenate([part[at : at + half] for part in wide], axis=0) for at in (0, half)
    ]


def finish_kernel(
    ids_ref, slot_ref, dropped_ref, gates_ref, out_grad_ref, *refs, exp_local
):
    parts, outs, (made, sems) = refs[:-5], refs[-5:-2], refs[-2:]
    mixed_ref, tok_grad_ref, gate_grad_ref = outs
    returned, returned_grad = [rows.astype(jnp.bfloat16) for rows in stack_halves(parts)]
    masks = slot_masks(ids_ref, slot_ref, dropped_ref, exp_local, returned.shape[0])
    select = sum(mask.astype(jnp.float32) for mask in masks).astype(jnp.bfloat16)
    made[0] = contract(select, returned_grad, 0, 0).astype(jnp.bfloat16)
    copies = [pltpu.make_async_copy(made.at[0], tok_grad_ref, sems.at[0])]
    copies[0].start()
    tokens = gates_ref.shape[1]
    gates = jnp.concatenate([gates_ref[...], jnp.zeros((6, tokens), jnp.float32)], axis=0).T
    wide = out_grad_ref[...].astype(jnp.float32)
    all_picked = [contract(mask.astype(jnp.bfloat16), returned, 0, 0) for mask in masks]
    mixed = sum(gates[:, k : k + 1] * picked for k, picked in enumerate(all_picked))
    made[1] = mixed.astype(jnp.bfloat16)
    copies.append(pltpu.make_async_copy(made.at[1], mixed_ref, sems.at[1]))
    copies[1].start()
    grads = [jnp.sum(picked * wide, axis=1, keepdims=True) for picked in all_picked]
    grads.append(jnp.zeros((tokens, 6), jnp.float32))
    gate_grad_ref[...] = jnp.concatenate(grads, axis=1).T[:2]
    for copy in copies:
        copy.wait()


def split_kernel(after_ref, *refs, exp_local):
    for out_ref, rows in zip(refs[-2:], stack_halves(refs[:-2])):
        order = order_matrix(exp_local, rows.shape[0])
        out_ref[...] = contract(order, rows.astype(jnp.bfloat16), 1, 0).astype(jnp.bfloat16)


def pair_kernel(*refs):
    own_ref, mate_ref, out_ref = refs[-3:]
    half = own_ref.shape[0]
    out_ref[:half] = own_ref[...]
    out_ref[half:] = mate_ref[...]


def pass_kernel(*refs):
    refs[-1][...] = refs[-2][...]


def add(left_ref, right_ref):
    total = left_ref[...].astype(jnp.float32) + right_ref[...].astype(jnp.float32)
    return total.astype(jnp.bfloat16)


def add_kernel(*refs):
    left_ref, right_ref = refs[-3:-1]
    refs[-1][...] = add(left_ref, right_ref)


def add_split_kernel(*refs):
    left_ref, right_ref, mine_ref, other_ref = refs[-4:]
    half = mine_ref.shape[0]
    total = add(left_ref, right_ref)
    mine_ref[...] = total[:half]
    other_ref[...] = total[half:]


def join_kernel(*refs, groups, exp_local):
    first_a, first_b, second_a, second_b = refs[-groups - 4 : -groups]
    order = order_matrix(exp_local, first_a.shape[0])
    first = contract(order, add(first_a, first_b), 0, 0)
    second = contract(order, add(second_a, second_b), 0, 0)
    half = first.shape[0] // groups
    for group, out_ref in enumerate(refs[-groups:]):
        part = slice(group * half, (group + 1) * half)
        out_ref[...] = jnp.concatenate([first[part], second[part]], axis=0).astype(jnp.bfloat16)


def hold_kernel(*refs):
    weight_ref, held_ref, done_ref, sems = refs[-4:]
    copies = [
        pltpu.make_async_copy(weight_ref.at[x], held_ref.at[x], sems.at[x])
        for x in range(weight_ref.shape[0])
    ]
    for copy in copies:
        copy.start()
    done_ref[...] = jnp.zeros(done_ref.shape, done_ref.dtype)
    for copy in copies:
        copy.wait()


def w_out_grad_kernel(*refs, skip, expert, at, chunk):
    hidden_ref, rows_ref = refs[skip : skip + 2]
    out_ref, done_ref, made, sems = refs[-4:]
    done_ref[...] = jnp.zeros(done_ref.shape, done_ref.dtype)
    copies = []
    for i, begin in enumerate(range(0, made.shape[0], chunk)):
        here, there = pl.ds(begin, chunk), pl.ds(at + begin, chunk)
        made[here] = contract(hidden_ref[expert, :, there], rows_ref[expert], 0, 0)
        copies.append(
            pltpu.make_async_copy(made.at[here], out_ref.at[expert, there], sems.at[i])
        )
        copies[-1].start()
    for copy in copies:
        copy.wait()


def w_in_grad_kernel(*refs, skip, expert, at, chunk):
    pre_grad_ref, rows_ref = refs[skip : skip + 2]
    out_ref, done_ref, made, sems = refs[-4:]
    done_ref[...] = jnp.zeros(done_ref.shape, done_ref.dtype)
    width, units = made.shape
    copies = []
    for i, begin in enumerate(range(0, width, chunk)):
        here = pl.ds(begin, min(chunk, width - begin))
        turned = rows_ref[expert, :, here].T
        made[here] = contract(turned, pre_grad_ref[expert, :, at : at + units], 1, 0)
        there = out_ref.at[expert, here, pl.ds(at, units)]
        copies.append(pltpu.make_async_copy(made.at[here], there, sems.at[i]))
        copies[-1].start()
    for copy in copies:
        copy.wait()


def params(rows):
    return pltpu.CompilerParams(vmem_limit_bytes=(6 << 20) + rows * (24 << 10))


def prepare(choices, gates, tokens, out_grad, groups, exp_local):
    block = (2 * exp_local * CAP, tokens.shape[1])
    whole = pl.BlockSpec(memory_space=pltpu.VMEM)
    return pl.pallas_call(
        functools.partial(prepare_kernel, exp_local=exp_local),
        out_specs=[whole] * groups,
        out_shape=[pltpu.VMEM(block, jnp.bfloat16)]
        + [jax.ShapeDtypeStruct(block, jnp.bfloat16)] * (groups - 1),
        compiler_params=pltpu.CompilerParams(vmem_limit_bytes=60 << 20),
        name="prepare",
    )(*choices, gates, tokens, out_grad)


def finish(choices, gates, out_grad, parts, exp_local):
    by_token = jax.ShapeDtypeStruct(out_grad.shape, jnp.bfloat16)
    anywhere = pl.BlockSpec(memory_space=pl.ANY)
    return pl.pallas_call(
        functools.partial(finish_kernel, exp_local=exp_local),
        out_specs=[anywhere, anywhere, pl.BlockSpec(memory_space=pltpu.VMEM)],
        out_shape=[by_token, by_token, jax.ShapeDtypeStruct(gates.shape, jnp.float32)],
        scratch_shapes=[
            pltpu.VMEM((2,) + out_grad.shape, jnp.bfloat16),
            pltpu.SemaphoreType.DMA((2,)),
        ],
        compiler_params=params(out_grad.shape[0]),
        name="finish",
    )(*choices, gates, out_grad, *parts)


def small_call(kernel, name, after, operands, counts):
    width = operands[0].shape[1]
    results = pl.pallas_call(
        kernel,
        in_specs=[pl.BlockSpec(memory_space=pl.ANY)] * len(after)
        + [pl.BlockSpec(memory_space=pltpu.VMEM)] * len(operands),
        out_shape=[jax.ShapeDtypeStruct((count, width), jnp.bfloat16) for count in counts],
        compiler_params=params(4 * counts[0]),
        cost_estimate=order_cost(counts[0], width),
        name=name,
    )(*after, *operands)
    return list(results)


def hold(after, weight):
    return pl.pallas_call(
        hold_kernel,
        in_specs=[pl.BlockSpec(memory_space=pl.ANY)] * (len(after) + 1),
        out_specs=[pl.BlockSpec(memory_space=pltpu.VMEM)] * 2,
        out_shape=[pltpu.VMEM(weight.shape, weight.dtype), DONE],
        scratch_shapes=[pltpu.SemaphoreType.DMA((weight.shape[0],))],
        compiler_params=pltpu.CompilerParams(vmem_limit_bytes=42 << 20),
        cost_estimate=pl.CostEstimate(
            flops=0, bytes_accessed=4 * weight.size, transcendentals=0
        ),
        name="hold",
    )(*after, weight)


def weight_gradient(kernel, hidden, rows, shape, after, name, expert, part, parts, base=None):
    whole = pl.BlockSpec(memory_space=pltpu.VMEM)
    anywhere = pl.BlockSpec(memory_space=pl.ANY)
    width, units = rows.shape[2], hidden.shape[2] // parts
    made, chunk = (width, units), CHUNK
    if kernel is w_out_grad_kernel:
        made, chunk = (units, width), min(CHUNK // 2, units)
    operands = (*after, hidden, rows) + (() if base is None else (base,))
    return pl.pallas_call(
        functools.partial(kernel, skip=len(after), expert=expert, at=part * units, chunk=chunk),
        in_specs=[anywhere] * len(after) + [whole] * 2 + [anywhere] * (base is not None),
        out_specs=[anywhere, whole],
        out_shape=[jax.ShapeDtypeStruct(shape, jnp.float32), DONE],
        input_output_aliases={} if base is None else {len(operands) - 1: 0},
        scratch_shapes=[
            pltpu.VMEM(made, jnp.float32),
            pltpu.SemaphoreType.DMA((-(-made[0] // chunk),)),
        ],
        compiler_params=pltpu.CompilerParams(vmem_limit_bytes=24 << 20),
        cost_estimate=pl.CostEstimate(
            flops=2 * rows.shape[1] * units * width,
            bytes_accessed=4 * units * width,
            transcendentals=0,
        ),
        name=name,
    )(*operands)


def sort_kernel(after_ref, *refs, places):
    blocks, out_ref = refs[:-1], refs[-1]
    experts = out_ref.shape[0]
    part = blocks[0].shape[0] // (2 * experts)
    for i, place in enumerate(places):
        for expert in range(experts):
            at = ((i % 2) * experts + expert) * part
            out_ref[expert, place * part : (place + 1) * part] = blocks[i // 2][at : at + part]


def unsort_kernel(after_ref, in_ref, *blocks):
    experts = in_ref.shape[0]
    part = blocks[0].shape[0] // (2 * experts)
    for i in range(2 * len(blocks)):
        for expert in range(experts):
            at = ((i % 2) * experts + expert) * part
            blocks[i // 2][at : at + part] = in_ref[expert, i * part : (i + 1) * part]


def backward_kernel(after_ref, *refs, places):
    blocks, (slope_ref, w_in_ref, w_out_ref) = refs[:-7], refs[-7:-4]
    rows_ref, pre_grad_ref, row_grad_ref, turned = refs[-4:]
    experts, units, width = w_out_ref.shape
    step = min(2 * CHUNK, units)
    sort_kernel(after_ref, *blocks, rows_ref, places=places)
    for expert in range(experts):
        grads = rows_ref[expert].T
        for at in range(0, units, step):
            here = slice(at, at + step)
            hidden_grad = contract(w_out_ref[expert, here], grads, 1, 0)
            pre_grad = (hidden_grad * slope_ref[expert, :, here].T).astype(jnp.bfloat16)
            turned[here] = pre_grad
            pre_grad_ref[expert, :, here] = pre_grad.T
        for at in range(0, width, CHUNK):
            here = slice(at, min(at + CHUNK, width))
            row_grad = contract(w_in_ref[expert, here], turned[...], 1, 0)
            row_grad_ref[expert, :, here] = row_grad.T.astype(jnp.bfloat16)


def order_cost(count, width):
    return pl.CostEstimate(
        flops=2 * count * count * width, bytes_accessed=4 * count * width, transcendentals=0
    )


def sort_rows(blocks, experts, places, after):
    count, width = blocks[0].shape
    rows = len(blocks) * count // experts
    return pl.pallas_call(
        functools.partial(sort_kernel, places=places),
        in_specs=[pl.BlockSpec(memory_space=pl.ANY)]
        + [pl.BlockSpec(memory_space=pltpu.VMEM)] * len(blocks),
        out_shape=jax.ShapeDtypeStruct((experts, rows, width), jnp.bfloat16),
        compiler_params=params(rows),
        cost_estimate=order_cost(experts * rows, width),
        name="sort_rows",
    )(after, *blocks)


def backward(blocks, slope, w_in, w_out, places, after):
    experts, units, width = w_out.shape
    rows = slope.shape[1]
    by_row = jax.ShapeDtypeStruct((experts, rows, width), jnp.bfloat16)
    return pl.pallas_call(
        functools.partial(backward_kernel, places=places),
        in_specs=[pl.BlockSpec(memory_space=pl.ANY)]
        + [pl.BlockSpec(memory_space=pltpu.VMEM)] * (len(blocks) + 3),
        out_shape=[by_row, jax.ShapeDtypeStruct(slope.shape, jnp.bfloat16), by_row],
        scratch_shapes=[pltpu.VMEM((units, rows), jnp.bfloat16)],
        compiler_params=pltpu.CompilerParams(vmem_limit_bytes=(10 << 20) + rows * (40 << 10)),
        cost_estimate=pl.CostEstimate(
            flops=4 * experts * rows * width * units,
            bytes_accessed=4 * experts * rows * width,
            transcendentals=0,
        ),
        name="backward",
    )(after, *blocks, slope, w_in, w_out)


def unsort_rows(rows, steps, after):
    experts, count, width = rows.shape
    block = experts * count // steps
    return pl.pallas_call(
        unsort_kernel,
        in_specs=[pl.BlockSpec(memory_space=pl.ANY), pl.BlockSpec(memory_space=pltpu.VMEM)],
        out_shape=[jax.ShapeDtypeStruct((block, width), jnp.bfloat16)] * steps,
        compiler_params=params(count),
        cost_estimate=order_cost(experts * count, width),
        name="unsort_rows",
    )(after, rows)


DP = ("far", "near", "pair")


def ring_mate(position, count, odd):
    if (position % 2 == 1) == odd:
        return (position + 1) % count
    return (position - 1) % count


def odd_edges(count):
    columns = count // 2
    ring = [2 * c for c in range(columns)] + [2 * c + 1 for c in reversed(range(columns))]
    return [(ring[i], ring[ring_mate(i, count, True)]) for i in range(count)]


def ring_order(count, odd):
    held = [[i, ring_mate(i, count, odd)] for i in range(count)]
    blocks = [list(pair) for pair in held]
    for _ in range(count // 2 - 1):
        odd = not odd
        held = [held[ring_mate(i, count, odd)] for i in range(count)]
        for mine, more in zip(blocks, held):
            mine += more
    return blocks


def regroup(count):
    even, odd = ring_order(count, False), ring_order(count, True)
    places = {tuple(e.index(block) for block in o) for e, o in zip(even, odd)}
    (place,) = places
    return place


def swap(block, odd):
    if odd:
        return lax.ppermute(block, DP, odd_edges(lax.axis_size(DP)))
    return lax.ppermute(block, "near", [(0, 1), (1, 0)])


def expert_swap(blocks):
    size = lax.axis_size("expert")
    got = [
        lax.ppermute(blocks[k], "expert", [(i, i ^ k) for i in range(size)])
        for k in reversed(range(1, size))
    ]
    return [blocks[0]] + got[::-1]


def per_device(tokens, expert_ids, slot_ids, dropped, gates, w_in, w_out, out_grad):
    n_expert = lax.axis_size("expert")
    n_dp = lax.axis_size(DP)
    steps = n_dp // 2
    exp_local = w_in.shape[0]
    count = n_expert * exp_local * CAP
    choices = (expert_ids.T, slot_ids.T, dropped.T)
    gates = gates.T
    send = prepare(choices, gates, tokens, out_grad, n_expert, exp_local)
    got = expert_swap(send)
    held_in, done_in = hold([], w_in)
    own_rows, own_grads = small_call(
        functools.partial(split_kernel, exp_local=exp_local), "split", [done_in], got, [count] * 2
    )

    mate_rows, mate_grads = swap(own_rows, False), swap(own_grads, True)
    pairs = [own_rows, mate_rows]
    row_blocks = small_call(pair_kernel, "pair", [mate_grads], pairs, [2 * count])
    pairs = [own_grads, mate_grads]
    grad_blocks = small_call(pair_kernel, "pair", [], pairs, [2 * count])
    held_out, done_out = hold([row_blocks[0], grad_blocks[0]], w_out)
    for step in range(1, steps):
        arrived = swap(row_blocks[-1], step % 2 == 1)
        if step == 1:
            (arrived,) = small_call(pass_kernel, "pass", [done_out], [arrived], [2 * count])
        row_blocks.append(arrived)
        grad_blocks.append(swap(grad_blocks[-1], step % 2 == 0))
    rows = sort_rows(row_blocks, exp_local, range(n_dp), done_in)
    pre = jnp.einsum("xmd,xdf->xmf", rows, held_in, preferred_element_type=jnp.float32)
    hidden = gelu_exact(pre).astype(jnp.bfloat16)
    output = jnp.einsum("xmf,xfd->xmd", hidden, held_out, preferred_element_type=jnp.float32)
    out_blocks = unsort_rows(output.astype(jnp.bfloat16), steps, done_out)
    grad_rows, pre_grad, row_grad = backward(
        grad_blocks, gelu_slope(pre), held_in, held_out, regroup(n_dp), out_blocks[-1]
    )

    def out_piece(expert, part, parts):
        return (w_out_grad_kernel, hidden, grad_rows, w_out.shape, expert, part, parts)

    def in_piece(expert, part, parts):
        return (w_in_grad_kernel, pre_grad, rows, w_in.shape, expert, part, parts)

    others, final = range(exp_local - 1), exp_local - 1
    work = [out_piece(x, 0, 1) for x in others] + [out_piece(final, part, 2) for part in (0, 1)]
    work += [in_piece(x, 0, 1) for x in range(exp_local)]
    made = {}

    def next_piece(after):
        if len(work) == 0:
            return after
        kernel, left, right, shape, expert, part, parts = work.pop(0)
        name = kernel.__name__
        made[name], ready = weight_gradient(
            kernel, left, right, shape, [after], name, expert, part, parts, made.get(name)
        )
        return ready

    def add_step(after, block, arrived, step):
        if step > 1:
            return small_call(add_kernel, "add", after, [block, arrived], [2 * count])
        return small_call(add_split_kernel, "add_split", after, [block, arrived], [count] * 2)

    last = steps - 1
    out_sum = out_blocks[last:]
    out_arrived = swap(out_sum[0], last % 2 == 1)
    for step in range(last, 0, -1):
        if step < last:
            back_arrived = swap(back_sum[-1], step % 2 == 1)
        ready = [next_piece(back_sum[-1])] if step == 1 < last else []
        out_sum = add_step(ready, out_blocks[step - 1], out_arrived, step)
        out_arrived = swap(out_sum[-1], step % 2 == 0)
        if step == last:
            back_blocks = unsort_rows(row_grad, steps, out_sum[0])
            back_sum = back_blocks[last:]
            back_arrived = swap(back_sum[-1], step % 2 == 1)
            ready = [next_piece(back_sum[-1])]
        elif step > 1:
            ready = [next_piece(out_sum[-1])]
        back_sum = add_step(ready, back_blocks[step - 1], back_arrived, step)
    back_arrived = swap(back_sum[-1], False)
    joined = small_call(
        functools.partial(join_kernel, groups=n_expert, exp_local=exp_local),
        "join",
        [next_piece(back_sum[-1])],
        [out_sum[0], out_arrived, back_sum[0], back_arrived],
        [2 * exp_local * CAP] * n_expert,
    )
    while work:
        next_piece(joined[0])
    mixed, tok_grad, gate_grad = finish(
        choices, gates, out_grad, expert_swap(joined), exp_local
    )
    return (mixed, tok_grad, gate_grad.T, made["w_in_grad_kernel"], made["w_out_grad_kernel"])


def solution(mesh):
    n_expert, n_dp = mesh.shape["expert"], mesh.shape["dp"]
    split = Mesh(mesh.devices.reshape(n_expert, n_dp // 4, 2, 2), ("expert",) + DP)
    rows = P(("expert",) + DP, None)
    into = P("expert", None, DP)
    out_of = P("expert", DP, None)
    return jax.shard_map(
        per_device,
        mesh=split,
        in_specs=(rows, rows, rows, rows, rows, into, out_of, rows),
        out_specs=(rows, rows, rows, into, out_of),
        check_vma=False,
    )
```

```python
import functools

import jax
import jax.numpy as jnp
from jax import lax
from jax.experimental import pallas as pl
from jax.experimental.pallas import tpu as pltpu
from jax.sharding import Mesh
from jax.sharding import PartitionSpec as P

CAP = 4
CHUNK = 256
DONE = jax.ShapeDtypeStruct((8, 128), jnp.float32)


inv_root_two = 0.7071067811865476
inv_root_two_pi = 0.3989422804014327


def gelu_exact(value):
    return 0.5 * value * (1.0 + lax.erf(value * inv_root_two))


def gelu_slope(value):
    return (
        0.5 * (1.0 + lax.erf(value * inv_root_two))
        + value * jnp.exp(-0.5 * value * value) * inv_root_two_pi
    )


def contract(left, right, left_dim, right_dim):
    return lax.dot_general(
        left,
        right,
        (((left_dim,), (right_dim,)), ((), ())),
        preferred_element_type=jnp.float32,
    )


def order_matrix(exp_local, count):
    pick = lax.broadcasted_iota(jnp.int32, (count, count), 0)
    row = lax.broadcasted_iota(jnp.int32, (count, count), 1)
    each = count // exp_local
    expert, rest = pick // each, pick % each
    wanted = (rest // CAP) * (CAP * exp_local) + expert * CAP + rest % CAP
    return (row == wanted).astype(jnp.bfloat16)


def slot_masks(ids_ref, slot_ref, dropped_ref, exp_local, columns):
    ids = ids_ref[...]
    group = jnp.bitwise_xor(ids // exp_local, lax.axis_index("expert"))
    target = (group * exp_local + ids % exp_local) * CAP + slot_ref[...]
    target = jnp.where(dropped_ref[...] == 0, target, -1)
    column = lax.broadcasted_iota(jnp.int32, (columns, target.shape[1]), 0)
    return [column == target[k : k + 1] for k in range(target.shape[0])]


def prepare_kernel(
    ids_ref, slot_ref, dropped_ref, gates_ref, tokens_ref, out_grad_ref, *outs, exp_local
):
    half = exp_local * CAP
    masks = slot_masks(ids_ref, slot_ref, dropped_ref, exp_local, half * len(outs))
    select = sum(mask.astype(jnp.float32) for mask in masks).astype(jnp.bfloat16)
    gate = sum(
        jnp.sum(jnp.where(mask, gates_ref[k : k + 1], 0.0), axis=1, keepdims=True)
        for k, mask in enumerate(masks)
    )
    rows = contract(select, tokens_ref[...], 1, 0)
    grads = contract(select, out_grad_ref[...], 1, 0) * gate
    for group, out_ref in enumerate(outs):
        part = slice(group * half, (group + 1) * half)
        out_ref[...] = jnp.concatenate([rows[part], grads[part]], axis=0).astype(jnp.bfloat16)


def stack_halves(refs):
    half = refs[0].shape[0] // 2
    wide = [ref[...].astype(jnp.float32) for ref in refs]
    return [
        jnp.concatenate([part[at : at + half] for part in wide], axis=0) for at in (0, half)
    ]


def finish_kernel(
    ids_ref, slot_ref, dropped_ref, gates_ref, out_grad_ref, *refs, exp_local
):
    parts, (mixed_ref, tok_grad_ref, gate_grad_ref) = refs[:-3], refs[-3:]
    returned, returned_grad = [rows.astype(jnp.bfloat16) for rows in stack_halves(parts)]
    masks = slot_masks(ids_ref, slot_ref, dropped_ref, exp_local, returned.shape[0])
    select = sum(mask.astype(jnp.float32) for mask in masks).astype(jnp.bfloat16)
    tok_grad_ref[...] = contract(select, returned_grad, 0, 0).astype(jnp.bfloat16)
    tokens = gates_ref.shape[1]
    gates = jnp.concatenate([gates_ref[...], jnp.zeros((6, tokens), jnp.float32)], axis=0).T
    wide = out_grad_ref[...].astype(jnp.float32)
    mixed = jnp.zeros(wide.shape, jnp.float32)
    grads = []
    for k, mask in enumerate(masks):
        picked = contract(mask.astype(jnp.bfloat16), returned, 0, 0)
        mixed = mixed + gates[:, k : k + 1] * picked
        grads.append(jnp.sum(picked * wide, axis=1, keepdims=True))
    mixed_ref[...] = mixed.astype(jnp.bfloat16)
    grads.append(jnp.zeros((tokens, 6), jnp.float32))
    gate_grad_ref[...] = jnp.concatenate(grads, axis=1).T[:2]


def split_kernel(after_ref, *refs, exp_local):
    for out_ref, rows in zip(refs[-2:], stack_halves(refs[:-2])):
        order = order_matrix(exp_local, rows.shape[0])
        out_ref[...] = contract(order, rows.astype(jnp.bfloat16), 1, 0).astype(jnp.bfloat16)


def pair_kernel(*refs):
    own_ref, mate_ref, out_ref = refs[-3:]
    half = own_ref.shape[0]
    out_ref[:half] = own_ref[...]
    out_ref[half:] = mate_ref[...]


def pass_kernel(*refs):
    refs[-1][...] = refs[-2][...]


def add(left_ref, right_ref):
    total = left_ref[...].astype(jnp.float32) + right_ref[...].astype(jnp.float32)
    return total.astype(jnp.bfloat16)


def add_kernel(*refs):
    left_ref, right_ref = refs[-3:-1]
    refs[-1][...] = add(left_ref, right_ref)


def add_split_kernel(*refs):
    left_ref, right_ref, mine_ref, other_ref = refs[-4:]
    half = mine_ref.shape[0]
    total = add(left_ref, right_ref)
    mine_ref[...] = total[:half]
    other_ref[...] = total[half:]


def join_kernel(*refs, groups, exp_local):
    first_a, first_b, second_a, second_b = refs[-groups - 4 : -groups]
    order = order_matrix(exp_local, first_a.shape[0])
    first = contract(order, add(first_a, first_b), 0, 0)
    second = contract(order, add(second_a, second_b), 0, 0)
    half = first.shape[0] // groups
    for group, out_ref in enumerate(refs[-groups:]):
        part = slice(group * half, (group + 1) * half)
        out_ref[...] = jnp.concatenate([first[part], second[part]], axis=0).astype(jnp.bfloat16)


def hold_kernel(*refs):
    weight_ref, held_ref, done_ref, sems = refs[-4:]
    copies = [
        pltpu.make_async_copy(weight_ref.at[x], held_ref.at[x], sems.at[x])
        for x in range(weight_ref.shape[0])
    ]
    for copy in copies:
        copy.start()
    done_ref[...] = jnp.zeros(done_ref.shape, done_ref.dtype)
    for copy in copies:
        copy.wait()


def w_out_grad_kernel(*refs, skip, expert, at, chunk):
    hidden_ref, rows_ref = refs[skip : skip + 2]
    out_ref, done_ref, made, sems = refs[-4:]
    done_ref[...] = jnp.zeros(done_ref.shape, done_ref.dtype)
    copies = []
    for i, begin in enumerate(range(0, made.shape[0], chunk)):
        here, there = pl.ds(begin, chunk), pl.ds(at + begin, chunk)
        made[here] = contract(hidden_ref[expert, :, there], rows_ref[expert], 0, 0)
        copies.append(
            pltpu.make_async_copy(made.at[here], out_ref.at[expert, there], sems.at[i])
        )
        copies[-1].start()
    for copy in copies:
        copy.wait()


def w_in_grad_kernel(*refs, skip, expert, at, chunk):
    pre_grad_ref, rows_ref = refs[skip : skip + 2]
    out_ref, done_ref, made, sems = refs[-4:]
    done_ref[...] = jnp.zeros(done_ref.shape, done_ref.dtype)
    width, units = made.shape
    copies = []
    for i, begin in enumerate(range(0, width, chunk)):
        here = pl.ds(begin, min(chunk, width - begin))
        turned = rows_ref[expert, :, here].T
        made[here] = contract(turned, pre_grad_ref[expert, :, at : at + units], 1, 0)
        there = out_ref.at[expert, here, pl.ds(at, units)]
        copies.append(pltpu.make_async_copy(made.at[here], there, sems.at[i]))
        copies[-1].start()
    for copy in copies:
        copy.wait()


def params(rows):
    return pltpu.CompilerParams(vmem_limit_bytes=(6 << 20) + rows * (24 << 10))


def prepare(choices, gates, tokens, out_grad, groups, exp_local):
    block = (2 * exp_local * CAP, tokens.shape[1])
    whole = pl.BlockSpec(memory_space=pltpu.VMEM)
    return pl.pallas_call(
        functools.partial(prepare_kernel, exp_local=exp_local),
        out_specs=[whole] * groups,
        out_shape=[pltpu.VMEM(block, jnp.bfloat16)]
        + [jax.ShapeDtypeStruct(block, jnp.bfloat16)] * (groups - 1),
        compiler_params=pltpu.CompilerParams(vmem_limit_bytes=60 << 20),
        name="prepare",
    )(*choices, gates, tokens, out_grad)


def finish(choices, gates, out_grad, parts, exp_local):
    return pl.pallas_call(
        functools.partial(finish_kernel, exp_local=exp_local),
        out_shape=[
            jax.ShapeDtypeStruct(out_grad.shape, jnp.bfloat16),
            jax.ShapeDtypeStruct(out_grad.shape, jnp.bfloat16),
            jax.ShapeDtypeStruct(gates.shape, jnp.float32),
        ],
        compiler_params=params(out_grad.shape[0]),
        name="finish",
    )(*choices, gates, out_grad, *parts)


def small_call(kernel, name, after, operands, counts):
    width = operands[0].shape[1]
    results = pl.pallas_call(
        kernel,
        in_specs=[pl.BlockSpec(memory_space=pl.ANY)] * len(after)
        + [pl.BlockSpec(memory_space=pltpu.VMEM)] * len(operands),
        out_shape=[jax.ShapeDtypeStruct((count, width), jnp.bfloat16) for count in counts],
        compiler_params=params(4 * counts[0]),
        cost_estimate=order_cost(counts[0], width),
        name=name,
    )(*after, *operands)
    return list(results)


def hold(after, weight):
    return pl.pallas_call(
        hold_kernel,
        in_specs=[pl.BlockSpec(memory_space=pl.ANY)] * (len(after) + 1),
        out_specs=[pl.BlockSpec(memory_space=pltpu.VMEM)] * 2,
        out_shape=[pltpu.VMEM(weight.shape, weight.dtype), DONE],
        scratch_shapes=[pltpu.SemaphoreType.DMA((weight.shape[0],))],
        compiler_params=pltpu.CompilerParams(vmem_limit_bytes=42 << 20),
        cost_estimate=pl.CostEstimate(
            flops=0, bytes_accessed=4 * weight.size, transcendentals=0
        ),
        name="hold",
    )(*after, weight)


def weight_gradient(kernel, hidden, rows, shape, after, name, expert, part, parts, base=None):
    whole = pl.BlockSpec(memory_space=pltpu.VMEM)
    anywhere = pl.BlockSpec(memory_space=pl.ANY)
    width, units = rows.shape[2], hidden.shape[2] // parts
    made, chunk = (width, units), CHUNK
    if kernel is w_out_grad_kernel:
        made, chunk = (units, width), min(CHUNK // 2, units)
    operands = (*after, hidden, rows) + (() if base is None else (base,))
    return pl.pallas_call(
        functools.partial(kernel, skip=len(after), expert=expert, at=part * units, chunk=chunk),
        in_specs=[anywhere] * len(after) + [whole] * 2 + [anywhere] * (base is not None),
        out_specs=[anywhere, whole],
        out_shape=[jax.ShapeDtypeStruct(shape, jnp.float32), DONE],
        input_output_aliases={} if base is None else {len(operands) - 1: 0},
        scratch_shapes=[
            pltpu.VMEM(made, jnp.float32),
            pltpu.SemaphoreType.DMA((-(-made[0] // chunk),)),
        ],
        compiler_params=pltpu.CompilerParams(vmem_limit_bytes=24 << 20),
        cost_estimate=pl.CostEstimate(
            flops=2 * rows.shape[1] * units * width,
            bytes_accessed=4 * units * width,
            transcendentals=0,
        ),
        name=name,
    )(*operands)


def sort_kernel(after_ref, *refs, places):
    blocks, out_ref = refs[:-1], refs[-1]
    experts = out_ref.shape[0]
    part = blocks[0].shape[0] // (2 * experts)
    for i, place in enumerate(places):
        for expert in range(experts):
            at = ((i % 2) * experts + expert) * part
            out_ref[expert, place * part : (place + 1) * part] = blocks[i // 2][at : at + part]


def unsort_kernel(after_ref, in_ref, *blocks):
    experts = in_ref.shape[0]
    part = blocks[0].shape[0] // (2 * experts)
    for i in range(2 * len(blocks)):
        for expert in range(experts):
            at = ((i % 2) * experts + expert) * part
            blocks[i // 2][at : at + part] = in_ref[expert, i * part : (i + 1) * part]


def order_cost(count, width):
    return pl.CostEstimate(
        flops=2 * count * count * width, bytes_accessed=4 * count * width, transcendentals=0
    )


def sort_rows(blocks, experts, places, after):
    count, width = blocks[0].shape
    rows = len(blocks) * count // experts
    return pl.pallas_call(
        functools.partial(sort_kernel, places=places),
        in_specs=[pl.BlockSpec(memory_space=pl.ANY)]
        + [pl.BlockSpec(memory_space=pltpu.VMEM)] * len(blocks),
        out_shape=jax.ShapeDtypeStruct((experts, rows, width), jnp.bfloat16),
        compiler_params=params(rows),
        cost_estimate=order_cost(experts * rows, width),
        name="sort_rows",
    )(after, *blocks)


def unsort_rows(rows, steps, after):
    experts, count, width = rows.shape
    block = experts * count // steps
    return pl.pallas_call(
        unsort_kernel,
        in_specs=[pl.BlockSpec(memory_space=pl.ANY), pl.BlockSpec(memory_space=pltpu.VMEM)],
        out_shape=[jax.ShapeDtypeStruct((block, width), jnp.bfloat16)] * steps,
        compiler_params=params(count),
        cost_estimate=order_cost(experts * count, width),
        name="unsort_rows",
    )(after, rows)


DP = ("far", "near", "pair")


def ring_mate(position, count, odd):
    if (position % 2 == 1) == odd:
        return (position + 1) % count
    return (position - 1) % count


def odd_edges(count):
    columns = count // 2
    ring = [2 * c for c in range(columns)] + [2 * c + 1 for c in reversed(range(columns))]
    return [(ring[i], ring[ring_mate(i, count, True)]) for i in range(count)]


def ring_order(count, odd):
    held = [[i, ring_mate(i, count, odd)] for i in range(count)]
    blocks = [list(pair) for pair in held]
    for _ in range(count // 2 - 1):
        odd = not odd
        held = [held[ring_mate(i, count, odd)] for i in range(count)]
        for mine, more in zip(blocks, held):
            mine += more
    return blocks


def regroup(count):
    even, odd = ring_order(count, False), ring_order(count, True)
    places = {tuple(e.index(block) for block in o) for e, o in zip(even, odd)}
    (place,) = places
    return place


def swap(block, odd):
    if odd:
        return lax.ppermute(block, DP, odd_edges(lax.axis_size(DP)))
    return lax.ppermute(block, "near", [(0, 1), (1, 0)])


def expert_swap(blocks):
    size = lax.axis_size("expert")
    got = [
        lax.ppermute(blocks[k], "expert", [(i, i ^ k) for i in range(size)])
        for k in reversed(range(1, size))
    ]
    return [blocks[0]] + got[::-1]


def per_device(tokens, expert_ids, slot_ids, dropped, gates, w_in, w_out, out_grad):
    n_expert = lax.axis_size("expert")
    n_dp = lax.axis_size(DP)
    steps = n_dp // 2
    exp_local = w_in.shape[0]
    count = n_expert * exp_local * CAP
    choices = (expert_ids.T, slot_ids.T, dropped.T)
    gates = gates.T
    send = prepare(choices, gates, tokens, out_grad, n_expert, exp_local)
    got = expert_swap(send)
    held_in, done_in = hold([], w_in)
    own_rows, own_grads = small_call(
        functools.partial(split_kernel, exp_local=exp_local), "split", [done_in], got, [count] * 2
    )

    mate_rows, mate_grads = swap(own_rows, False), swap(own_grads, True)
    pairs = [own_rows, mate_rows]
    row_blocks = small_call(pair_kernel, "pair", [mate_grads], pairs, [2 * count])
    pairs = [own_grads, mate_grads]
    grad_blocks = small_call(pair_kernel, "pair", [], pairs, [2 * count])
    held_out, done_out = hold([row_blocks[0], grad_blocks[0]], w_out)
    for step in range(1, steps):
        arrived = swap(row_blocks[-1], step % 2 == 1)
        if step == 1:
            (arrived,) = small_call(pass_kernel, "pass", [done_out], [arrived], [2 * count])
        row_blocks.append(arrived)
        grad_blocks.append(swap(grad_blocks[-1], step % 2 == 0))
    rows = sort_rows(row_blocks, exp_local, range(n_dp), done_in)
    pre = jnp.einsum("xmd,xdf->xmf", rows, held_in, preferred_element_type=jnp.float32)
    hidden = gelu_exact(pre).astype(jnp.bfloat16)
    output = jnp.einsum("xmf,xfd->xmd", hidden, held_out, preferred_element_type=jnp.float32)
    out_blocks = unsort_rows(output.astype(jnp.bfloat16), steps, done_out)
    grad_rows = sort_rows(grad_blocks, exp_local, regroup(n_dp), out_blocks[-1])
    hidden_grad = jnp.einsum(
        "xmd,xfd->xmf", grad_rows, held_out, preferred_element_type=jnp.float32
    )
    pre_grad = (hidden_grad * gelu_slope(pre)).astype(jnp.bfloat16)
    row_grad = jnp.einsum(
        "xmf,xdf->xmd", pre_grad, held_in, preferred_element_type=jnp.float32
    )

    def out_piece(expert, part, parts):
        return (w_out_grad_kernel, hidden, grad_rows, w_out.shape, expert, part, parts)

    def in_piece(expert, part, parts):
        return (w_in_grad_kernel, pre_grad, rows, w_in.shape, expert, part, parts)

    others, final = range(exp_local - 1), exp_local - 1
    work = [out_piece(x, 0, 1) for x in others] + [out_piece(final, 0, 2)]
    work += [in_piece(x, 0, 1) for x in others] + [out_piece(final, 1, 2), in_piece(final, 0, 1)]
    made = {}

    def next_piece(after):
        if len(work) == 0:
            return after
        kernel, left, right, shape, expert, part, parts = work.pop(0)
        name = kernel.__name__
        made[name], ready = weight_gradient(
            kernel, left, right, shape, [after], name, expert, part, parts, made.get(name)
        )
        return ready

    def add_step(after, block, arrived, step):
        if step > 1:
            return small_call(add_kernel, "add", after, [block, arrived], [2 * count])
        return small_call(add_split_kernel, "add_split", after, [block, arrived], [count] * 2)

    last = steps - 1
    out_sum = out_blocks[last:]
    out_arrived = swap(out_sum[0], last % 2 == 1)
    for step in range(last, 0, -1):
        if step < last:
            back_arrived = swap(back_sum[-1], step % 2 == 1)
        ready = [next_piece(back_sum[-1])] if step == 1 < last else []
        out_sum = add_step(ready, out_blocks[step - 1], out_arrived, step)
        out_arrived = swap(out_sum[-1], step % 2 == 0)
        if step == last:
            back_blocks = unsort_rows(row_grad.astype(jnp.bfloat16), steps, out_sum[0])
            back_sum = back_blocks[last:]
            back_arrived = swap(back_sum[-1], step % 2 == 1)
            ready = [next_piece(back_sum[-1])]
        elif step > 1:
            ready = [next_piece(out_sum[-1])]
        back_sum = add_step(ready, back_blocks[step - 1], back_arrived, step)
    back_arrived = swap(back_sum[-1], False)
    joined = small_call(
        functools.partial(join_kernel, groups=n_expert, exp_local=exp_local),
        "join",
        [next_piece(back_sum[-1])],
        [out_sum[0], out_arrived, back_sum[0], back_arrived],
        [2 * exp_local * CAP] * n_expert,
    )
    while work:
        next_piece(joined[0])
    mixed, tok_grad, gate_grad = finish(
        choices, gates, out_grad, expert_swap(joined), exp_local
    )
    return (mixed, tok_grad, gate_grad.T, made["w_in_grad_kernel"], made["w_out_grad_kernel"])


def solution(mesh):
    n_expert, n_dp = mesh.shape["expert"], mesh.shape["dp"]
    split = Mesh(mesh.devices.reshape(n_expert, n_dp // 4, 2, 2), ("expert",) + DP)
    rows = P(("expert",) + DP, None)
    into = P("expert", None, DP)
    out_of = P("expert", DP, None)
    return jax.shard_map(
        per_device,
        mesh=split,
        in_specs=(rows, rows, rows, rows, rows, into, out_of, rows),
        out_specs=(rows, rows, rows, into, out_of),
        check_vma=False,
    )
```

```python
import functools

import jax
import jax.numpy as jnp
from jax import lax
from jax.experimental import pallas as pl
from jax.experimental.pallas import tpu as pltpu
from jax.sharding import Mesh
from jax.sharding import PartitionSpec as P

CAP = 4
CHUNK = 256
DONE = jax.ShapeDtypeStruct((8, 128), jnp.float32)


inv_root_two = 0.7071067811865476
inv_root_two_pi = 0.3989422804014327


def gelu_exact(value):
    return 0.5 * value * (1.0 + lax.erf(value * inv_root_two))


def gelu_slope(value):
    return (
        0.5 * (1.0 + lax.erf(value * inv_root_two))
        + value * jnp.exp(-0.5 * value * value) * inv_root_two_pi
    )


def contract(left, right, left_dim, right_dim):
    return lax.dot_general(
        left,
        right,
        (((left_dim,), (right_dim,)), ((), ())),
        preferred_element_type=jnp.float32,
    )


def order_matrix(exp_local, count):
    pick = lax.broadcasted_iota(jnp.int32, (count, count), 0)
    row = lax.broadcasted_iota(jnp.int32, (count, count), 1)
    each = count // exp_local
    expert, rest = pick // each, pick % each
    wanted = (rest // CAP) * (CAP * exp_local) + expert * CAP + rest % CAP
    return (row == wanted).astype(jnp.bfloat16)


def slot_masks(ids_ref, slot_ref, dropped_ref, exp_local, columns):
    ids = ids_ref[...]
    group = jnp.bitwise_xor(ids // exp_local, lax.axis_index("expert"))
    target = (group * exp_local + ids % exp_local) * CAP + slot_ref[...]
    target = jnp.where(dropped_ref[...] == 0, target, -1)
    column = lax.broadcasted_iota(jnp.int32, (columns, target.shape[1]), 0)
    return [column == target[k : k + 1] for k in range(target.shape[0])]


def prepare_kernel(
    ids_ref, slot_ref, dropped_ref, gates_ref, tokens_ref, out_grad_ref, *outs, exp_local
):
    half = exp_local * CAP
    masks = slot_masks(ids_ref, slot_ref, dropped_ref, exp_local, half * len(outs))
    select = sum(mask.astype(jnp.float32) for mask in masks).astype(jnp.bfloat16)
    gate = sum(
        jnp.sum(jnp.where(mask, gates_ref[k : k + 1], 0.0), axis=1, keepdims=True)
        for k, mask in enumerate(masks)
    )
    rows = contract(select, tokens_ref[...], 1, 0)
    grads = contract(select, out_grad_ref[...], 1, 0) * gate
    for group, out_ref in enumerate(outs):
        part = slice(group * half, (group + 1) * half)
        out_ref[...] = jnp.concatenate([rows[part], grads[part]], axis=0).astype(jnp.bfloat16)


def stack_halves(refs):
    half = refs[0].shape[0] // 2
    wide = [ref[...].astype(jnp.float32) for ref in refs]
    return [
        jnp.concatenate([part[at : at + half] for part in wide], axis=0) for at in (0, half)
    ]


def finish_kernel(
    ids_ref, slot_ref, dropped_ref, gates_ref, out_grad_ref, *refs, exp_local
):
    parts, (mixed_ref, tok_grad_ref, gate_grad_ref) = refs[:-3], refs[-3:]
    returned, returned_grad = [rows.astype(jnp.bfloat16) for rows in stack_halves(parts)]
    masks = slot_masks(ids_ref, slot_ref, dropped_ref, exp_local, returned.shape[0])
    select = sum(mask.astype(jnp.float32) for mask in masks).astype(jnp.bfloat16)
    tok_grad_ref[...] = contract(select, returned_grad, 0, 0).astype(jnp.bfloat16)
    tokens = gates_ref.shape[1]
    gates = jnp.concatenate([gates_ref[...], jnp.zeros((6, tokens), jnp.float32)], axis=0).T
    wide = out_grad_ref[...].astype(jnp.float32)
    mixed = jnp.zeros(wide.shape, jnp.float32)
    grads = []
    for k, mask in enumerate(masks):
        picked = contract(mask.astype(jnp.bfloat16), returned, 0, 0)
        mixed = mixed + gates[:, k : k + 1] * picked
        grads.append(jnp.sum(picked * wide, axis=1, keepdims=True))
    mixed_ref[...] = mixed.astype(jnp.bfloat16)
    grads.append(jnp.zeros((tokens, 6), jnp.float32))
    gate_grad_ref[...] = jnp.concatenate(grads, axis=1).T[:2]


def split_kernel(after_ref, *refs, exp_local):
    for out_ref, rows in zip(refs[-2:], stack_halves(refs[:-2])):
        order = order_matrix(exp_local, rows.shape[0])
        out_ref[...] = contract(order, rows.astype(jnp.bfloat16), 1, 0).astype(jnp.bfloat16)


def pair_kernel(*refs):
    own_ref, mate_ref, out_ref = refs[-3:]
    half = own_ref.shape[0]
    out_ref[:half] = own_ref[...]
    out_ref[half:] = mate_ref[...]


def pass_kernel(*refs):
    refs[-1][...] = refs[-2][...]


def add(left_ref, right_ref):
    total = left_ref[...].astype(jnp.float32) + right_ref[...].astype(jnp.float32)
    return total.astype(jnp.bfloat16)


def add_kernel(*refs):
    left_ref, right_ref = refs[-3:-1]
    refs[-1][...] = add(left_ref, right_ref)


def add_split_kernel(*refs):
    left_ref, right_ref, mine_ref, other_ref = refs[-4:]
    half = mine_ref.shape[0]
    total = add(left_ref, right_ref)
    mine_ref[...] = total[:half]
    other_ref[...] = total[half:]


def join_kernel(*refs, groups, exp_local):
    first_a, first_b, second_a, second_b = refs[-groups - 4 : -groups]
    order = order_matrix(exp_local, first_a.shape[0])
    first = contract(order, add(first_a, first_b), 0, 0)
    second = contract(order, add(second_a, second_b), 0, 0)
    half = first.shape[0] // groups
    for group, out_ref in enumerate(refs[-groups:]):
        part = slice(group * half, (group + 1) * half)
        out_ref[...] = jnp.concatenate([first[part], second[part]], axis=0).astype(jnp.bfloat16)


def hold_kernel(*refs):
    weight_ref, held_ref, done_ref, sems = refs[-4:]
    copies = [
        pltpu.make_async_copy(weight_ref.at[x], held_ref.at[x], sems.at[x])
        for x in range(weight_ref.shape[0])
    ]
    for copy in copies:
        copy.start()
    done_ref[...] = jnp.zeros(done_ref.shape, done_ref.dtype)
    for copy in copies:
        copy.wait()


def w_out_grad_kernel(*refs, skip, expert, at, chunk):
    hidden_ref, rows_ref = refs[skip : skip + 2]
    out_ref, done_ref, made, sems = refs[-4:]
    done_ref[...] = jnp.zeros(done_ref.shape, done_ref.dtype)
    copies = []
    for i, begin in enumerate(range(0, made.shape[0], chunk)):
        here, there = pl.ds(begin, chunk), pl.ds(at + begin, chunk)
        made[here] = contract(hidden_ref[expert, :, there], rows_ref[expert], 0, 0)
        copies.append(
            pltpu.make_async_copy(made.at[here], out_ref.at[expert, there], sems.at[i])
        )
        copies[-1].start()
    for copy in copies:
        copy.wait()


def w_in_grad_kernel(*refs, skip, expert, at, chunk):
    pre_grad_ref, rows_ref = refs[skip : skip + 2]
    out_ref, done_ref, made, sems = refs[-4:]
    done_ref[...] = jnp.zeros(done_ref.shape, done_ref.dtype)
    width, units = made.shape
    copies = []
    for i, begin in enumerate(range(0, width, chunk)):
        here = pl.ds(begin, min(chunk, width - begin))
        turned = rows_ref[expert, :, here].T
        made[here] = contract(turned, pre_grad_ref[expert, :, at : at + units], 1, 0)
        there = out_ref.at[expert, here, pl.ds(at, units)]
        copies.append(pltpu.make_async_copy(made.at[here], there, sems.at[i]))
        copies[-1].start()
    for copy in copies:
        copy.wait()


def params(rows):
    return pltpu.CompilerParams(vmem_limit_bytes=(6 << 20) + rows * (24 << 10))


def prepare(choices, gates, tokens, out_grad, groups, exp_local):
    block = (2 * exp_local * CAP, tokens.shape[1])
    whole = pl.BlockSpec(memory_space=pltpu.VMEM)
    return pl.pallas_call(
        functools.partial(prepare_kernel, exp_local=exp_local),
        out_specs=[whole] * groups,
        out_shape=[pltpu.VMEM(block, jnp.bfloat16)]
        + [jax.ShapeDtypeStruct(block, jnp.bfloat16)] * (groups - 1),
        compiler_params=pltpu.CompilerParams(vmem_limit_bytes=60 << 20),
        name="prepare",
    )(*choices, gates, tokens, out_grad)


def finish(choices, gates, out_grad, parts, exp_local):
    return pl.pallas_call(
        functools.partial(finish_kernel, exp_local=exp_local),
        out_shape=[
            jax.ShapeDtypeStruct(out_grad.shape, jnp.bfloat16),
            jax.ShapeDtypeStruct(out_grad.shape, jnp.bfloat16),
            jax.ShapeDtypeStruct(gates.shape, jnp.float32),
        ],
        compiler_params=params(out_grad.shape[0]),
        name="finish",
    )(*choices, gates, out_grad, *parts)


def small_call(kernel, name, after, operands, counts):
    width = operands[0].shape[1]
    results = pl.pallas_call(
        kernel,
        in_specs=[pl.BlockSpec(memory_space=pl.ANY)] * len(after)
        + [pl.BlockSpec(memory_space=pltpu.VMEM)] * len(operands),
        out_shape=[jax.ShapeDtypeStruct((count, width), jnp.bfloat16) for count in counts],
        compiler_params=params(4 * counts[0]),
        cost_estimate=order_cost(counts[0], width),
        name=name,
    )(*after, *operands)
    return list(results)


def hold(after, weight):
    return pl.pallas_call(
        hold_kernel,
        in_specs=[pl.BlockSpec(memory_space=pl.ANY)] * (len(after) + 1),
        out_specs=[pl.BlockSpec(memory_space=pltpu.VMEM)] * 2,
        out_shape=[pltpu.VMEM(weight.shape, weight.dtype), DONE],
        scratch_shapes=[pltpu.SemaphoreType.DMA((weight.shape[0],))],
        compiler_params=pltpu.CompilerParams(vmem_limit_bytes=42 << 20),
        cost_estimate=pl.CostEstimate(
            flops=0, bytes_accessed=4 * weight.size, transcendentals=0
        ),
        name="hold",
    )(*after, weight)


def weight_gradient(kernel, hidden, rows, shape, after, name, expert, part, parts, base=None):
    whole = pl.BlockSpec(memory_space=pltpu.VMEM)
    anywhere = pl.BlockSpec(memory_space=pl.ANY)
    width, units = rows.shape[2], hidden.shape[2] // parts
    made, chunk = (width, units), CHUNK
    if kernel is w_out_grad_kernel:
        made, chunk = (units, width), min(CHUNK // 2, units)
    operands = (*after, hidden, rows) + (() if base is None else (base,))
    return pl.pallas_call(
        functools.partial(kernel, skip=len(after), expert=expert, at=part * units, chunk=chunk),
        in_specs=[anywhere] * len(after) + [whole] * 2 + [anywhere] * (base is not None),
        out_specs=[anywhere, whole],
        out_shape=[jax.ShapeDtypeStruct(shape, jnp.float32), DONE],
        input_output_aliases={} if base is None else {len(operands) - 1: 0},
        scratch_shapes=[
            pltpu.VMEM(made, jnp.float32),
            pltpu.SemaphoreType.DMA((-(-made[0] // chunk),)),
        ],
        compiler_params=pltpu.CompilerParams(vmem_limit_bytes=24 << 20),
        cost_estimate=pl.CostEstimate(
            flops=2 * rows.shape[1] * units * width,
            bytes_accessed=4 * units * width,
            transcendentals=0,
        ),
        name=name,
    )(*operands)


def sort_kernel(after_ref, *refs, places):
    blocks, out_ref = refs[:-1], refs[-1]
    experts = out_ref.shape[0]
    part = blocks[0].shape[0] // (2 * experts)
    for i, place in enumerate(places):
        for expert in range(experts):
            at = ((i % 2) * experts + expert) * part
            out_ref[expert, place * part : (place + 1) * part] = blocks[i // 2][at : at + part]


def unsort_kernel(after_ref, in_ref, *blocks):
    experts = in_ref.shape[0]
    part = blocks[0].shape[0] // (2 * experts)
    for i in range(2 * len(blocks)):
        for expert in range(experts):
            at = ((i % 2) * experts + expert) * part
            blocks[i // 2][at : at + part] = in_ref[expert, i * part : (i + 1) * part]


def backward_kernel(after_ref, *refs, places):
    blocks, (slope_ref, w_in_ref, w_out_ref) = refs[:-7], refs[-7:-4]
    rows_ref, pre_grad_ref, row_grad_ref, turned = refs[-4:]
    experts, units, width = w_out_ref.shape
    step = min(2 * CHUNK, units)
    sort_kernel(after_ref, *blocks, rows_ref, places=places)
    for expert in range(experts):
        grads = rows_ref[expert].T
        for at in range(0, units, step):
            here = slice(at, at + step)
            hidden_grad = contract(w_out_ref[expert, here], grads, 1, 0)
            pre_grad = (hidden_grad * slope_ref[expert, :, here].T).astype(jnp.bfloat16)
            turned[here] = pre_grad
            pre_grad_ref[expert, :, here] = pre_grad.T
        for at in range(0, width, CHUNK):
            here = slice(at, min(at + CHUNK, width))
            row_grad = contract(w_in_ref[expert, here], turned[...], 1, 0)
            row_grad_ref[expert, :, here] = row_grad.T.astype(jnp.bfloat16)


def order_cost(count, width):
    return pl.CostEstimate(
        flops=2 * count * count * width, bytes_accessed=4 * count * width, transcendentals=0
    )


def sort_rows(blocks, experts, places, after):
    count, width = blocks[0].shape
    rows = len(blocks) * count // experts
    return pl.pallas_call(
        functools.partial(sort_kernel, places=places),
        in_specs=[pl.BlockSpec(memory_space=pl.ANY)]
        + [pl.BlockSpec(memory_space=pltpu.VMEM)] * len(blocks),
        out_shape=jax.ShapeDtypeStruct((experts, rows, width), jnp.bfloat16),
        compiler_params=params(rows),
        cost_estimate=order_cost(experts * rows, width),
        name="sort_rows",
    )(after, *blocks)


def backward(blocks, slope, w_in, w_out, places, after):
    experts, units, width = w_out.shape
    rows = slope.shape[1]
    by_row = jax.ShapeDtypeStruct((experts, rows, width), jnp.bfloat16)
    return pl.pallas_call(
        functools.partial(backward_kernel, places=places),
        in_specs=[pl.BlockSpec(memory_space=pl.ANY)]
        + [pl.BlockSpec(memory_space=pltpu.VMEM)] * (len(blocks) + 3),
        out_shape=[by_row, jax.ShapeDtypeStruct(slope.shape, jnp.bfloat16), by_row],
        scratch_shapes=[pltpu.VMEM((units, rows), jnp.bfloat16)],
        compiler_params=pltpu.CompilerParams(vmem_limit_bytes=(10 << 20) + rows * (40 << 10)),
        cost_estimate=pl.CostEstimate(
            flops=4 * experts * rows * width * units,
            bytes_accessed=4 * experts * rows * width,
            transcendentals=0,
        ),
        name="backward",
    )(after, *blocks, slope, w_in, w_out)


def unsort_rows(rows, steps, after):
    experts, count, width = rows.shape
    block = experts * count // steps
    return pl.pallas_call(
        unsort_kernel,
        in_specs=[pl.BlockSpec(memory_space=pl.ANY), pl.BlockSpec(memory_space=pltpu.VMEM)],
        out_shape=[jax.ShapeDtypeStruct((block, width), jnp.bfloat16)] * steps,
        compiler_params=params(count),
        cost_estimate=order_cost(experts * count, width),
        name="unsort_rows",
    )(after, rows)


DP = ("far", "near", "pair")


def ring_mate(position, count, odd):
    if (position % 2 == 1) == odd:
        return (position + 1) % count
    return (position - 1) % count


def odd_edges(count):
    columns = count // 2
    ring = [2 * c for c in range(columns)] + [2 * c + 1 for c in reversed(range(columns))]
    return [(ring[i], ring[ring_mate(i, count, True)]) for i in range(count)]


def ring_order(count, odd):
    held = [[i, ring_mate(i, count, odd)] for i in range(count)]
    blocks = [list(pair) for pair in held]
    for _ in range(count // 2 - 1):
        odd = not odd
        held = [held[ring_mate(i, count, odd)] for i in range(count)]
        for mine, more in zip(blocks, held):
            mine += more
    return blocks


def regroup(count):
    even, odd = ring_order(count, False), ring_order(count, True)
    places = {tuple(e.index(block) for block in o) for e, o in zip(even, odd)}
    (place,) = places
    return place


def swap(block, odd):
    if odd:
        return lax.ppermute(block, DP, odd_edges(lax.axis_size(DP)))
    return lax.ppermute(block, "near", [(0, 1), (1, 0)])


def expert_swap(blocks):
    size = lax.axis_size("expert")
    got = [
        lax.ppermute(blocks[k], "expert", [(i, i ^ k) for i in range(size)])
        for k in reversed(range(1, size))
    ]
    return [blocks[0]] + got[::-1]


def per_device(tokens, expert_ids, slot_ids, dropped, gates, w_in, w_out, out_grad):
    n_expert = lax.axis_size("expert")
    n_dp = lax.axis_size(DP)
    steps = n_dp // 2
    exp_local = w_in.shape[0]
    count = n_expert * exp_local * CAP
    choices = (expert_ids.T, slot_ids.T, dropped.T)
    gates = gates.T
    send = prepare(choices, gates, tokens, out_grad, n_expert, exp_local)
    got = expert_swap(send)
    held_in, done_in = hold([], w_in)
    own_rows, own_grads = small_call(
        functools.partial(split_kernel, exp_local=exp_local), "split", [done_in], got, [count] * 2
    )

    mate_rows, mate_grads = swap(own_rows, False), swap(own_grads, True)
    pairs = [own_rows, mate_rows]
    row_blocks = small_call(pair_kernel, "pair", [mate_grads], pairs, [2 * count])
    pairs = [own_grads, mate_grads]
    grad_blocks = small_call(pair_kernel, "pair", [], pairs, [2 * count])
    held_out, done_out = hold([row_blocks[0], grad_blocks[0]], w_out)
    for step in range(1, steps):
        arrived = swap(row_blocks[-1], step % 2 == 1)
        if step == 1:
            (arrived,) = small_call(pass_kernel, "pass", [done_out], [arrived], [2 * count])
        row_blocks.append(arrived)
        grad_blocks.append(swap(grad_blocks[-1], step % 2 == 0))
    rows = sort_rows(row_blocks, exp_local, range(n_dp), done_in)
    pre = jnp.einsum("xmd,xdf->xmf", rows, held_in, preferred_element_type=jnp.float32)
    hidden = gelu_exact(pre).astype(jnp.bfloat16)
    output = jnp.einsum("xmf,xfd->xmd", hidden, held_out, preferred_element_type=jnp.float32)
    out_blocks = unsort_rows(output.astype(jnp.bfloat16), steps, done_out)
    grad_rows, pre_grad, row_grad = backward(
        grad_blocks, gelu_slope(pre), held_in, held_out, regroup(n_dp), out_blocks[-1]
    )
    back_blocks = unsort_rows(row_grad, steps, done_out)

    def out_piece(expert, part, parts):
        return (w_out_grad_kernel, hidden, grad_rows, w_out.shape, expert, part, parts)

    def in_piece(expert, part, parts):
        return (w_in_grad_kernel, pre_grad, rows, w_in.shape, expert, part, parts)

    others, final = range(exp_local - 1), exp_local - 1
    work = [out_piece(x, 0, 1) for x in others] + [out_piece(final, 0, 2)]
    work += [in_piece(x, 0, 1) for x in others] + [out_piece(final, 1, 2), in_piece(final, 0, 1)]
    made = {}

    def next_piece(after):
        if len(work) == 0:
            return after
        kernel, left, right, shape, expert, part, parts = work.pop(0)
        name = kernel.__name__
        made[name], ready = weight_gradient(
            kernel, left, right, shape, [after], name, expert, part, parts, made.get(name)
        )
        return ready

    def add_step(after, block, arrived, step):
        if step > 1:
            return small_call(add_kernel, "add", after, [block, arrived], [2 * count])
        return small_call(add_split_kernel, "add_split", after, [block, arrived], [count] * 2)

    last = steps - 1
    out_sum = out_blocks[last:]
    out_arrived = swap(out_sum[0], last % 2 == 1)
    for step in range(last, 0, -1):
        if step < last:
            back_arrived = swap(back_sum[-1], step % 2 == 1)
        ready = [next_piece(back_sum[-1])] if step == 1 < last else []
        out_sum = add_step(ready, out_blocks[step - 1], out_arrived, step)
        out_arrived = swap(out_sum[-1], step % 2 == 0)
        if step == last:
            back_sum = back_blocks[last:]
            back_arrived = swap(back_sum[-1], step % 2 == 1)
            ready = [next_piece(back_sum[-1])]
        elif step > 1:
            ready = [next_piece(out_sum[-1])]
        back_sum = add_step(ready, back_blocks[step - 1], back_arrived, step)
    back_arrived = swap(back_sum[-1], False)
    joined = small_call(
        functools.partial(join_kernel, groups=n_expert, exp_local=exp_local),
        "join",
        [next_piece(back_sum[-1])],
        [out_sum[0], out_arrived, back_sum[0], back_arrived],
        [2 * exp_local * CAP] * n_expert,
    )
    while work:
        next_piece(joined[0])
    mixed, tok_grad, gate_grad = finish(
        choices, gates, out_grad, expert_swap(joined), exp_local
    )
    return (mixed, tok_grad, gate_grad.T, made["w_in_grad_kernel"], made["w_out_grad_kernel"])


def solution(mesh):
    n_expert, n_dp = mesh.shape["expert"], mesh.shape["dp"]
    split = Mesh(mesh.devices.reshape(n_expert, n_dp // 4, 2, 2), ("expert",) + DP)
    rows = P(("expert",) + DP, None)
    into = P("expert", None, DP)
    out_of = P("expert", DP, None)
    return jax.shard_map(
        per_device,
        mesh=split,
        in_specs=(rows, rows, rows, rows, rows, into, out_of, rows),
        out_specs=(rows, rows, rows, into, out_of),
        check_vma=False,
    )
```

```python
import functools

import jax
import jax.numpy as jnp
from jax import lax
from jax.experimental import pallas as pl
from jax.experimental.pallas import tpu as pltpu
from jax.sharding import Mesh
from jax.sharding import PartitionSpec as P

CAP = 4
CHUNK = 256
DONE = jax.ShapeDtypeStruct((8, 128), jnp.float32)


inv_root_two = 0.7071067811865476
inv_root_two_pi = 0.3989422804014327


def gelu_exact(value):
    return 0.5 * value * (1.0 + lax.erf(value * inv_root_two))


def gelu_slope(value):
    return (
        0.5 * (1.0 + lax.erf(value * inv_root_two))
        + value * jnp.exp(-0.5 * value * value) * inv_root_two_pi
    )


def contract(left, right, left_dim, right_dim):
    return lax.dot_general(
        left,
        right,
        (((left_dim,), (right_dim,)), ((), ())),
        preferred_element_type=jnp.float32,
    )


def order_matrix(exp_local, count):
    pick = lax.broadcasted_iota(jnp.int32, (count, count), 0)
    row = lax.broadcasted_iota(jnp.int32, (count, count), 1)
    each = count // exp_local
    expert, rest = pick // each, pick % each
    wanted = (rest // CAP) * (CAP * exp_local) + expert * CAP + rest % CAP
    return (row == wanted).astype(jnp.bfloat16)


def slot_masks(ids_ref, slot_ref, dropped_ref, exp_local, columns):
    ids = ids_ref[...]
    group = jnp.bitwise_xor(ids // exp_local, lax.axis_index("expert"))
    target = (group * exp_local + ids % exp_local) * CAP + slot_ref[...]
    target = jnp.where(dropped_ref[...] == 0, target, -1)
    column = lax.broadcasted_iota(jnp.int32, (columns, target.shape[1]), 0)
    return [column == target[k : k + 1] for k in range(target.shape[0])]


def prepare_kernel(
    ids_ref, slot_ref, dropped_ref, gates_ref, tokens_ref, out_grad_ref, *outs, exp_local
):
    half = exp_local * CAP
    masks = slot_masks(ids_ref, slot_ref, dropped_ref, exp_local, half * len(outs))
    select = sum(mask.astype(jnp.float32) for mask in masks).astype(jnp.bfloat16)
    gate = sum(
        jnp.sum(jnp.where(mask, gates_ref[k : k + 1], 0.0), axis=1, keepdims=True)
        for k, mask in enumerate(masks)
    )
    rows = contract(select, tokens_ref[...], 1, 0)
    grads = contract(select, out_grad_ref[...], 1, 0) * gate
    for group, out_ref in enumerate(outs):
        part = slice(group * half, (group + 1) * half)
        out_ref[...] = jnp.concatenate([rows[part], grads[part]], axis=0).astype(jnp.bfloat16)


def stack_halves(refs):
    half = refs[0].shape[0] // 2
    wide = [ref[...].astype(jnp.float32) for ref in refs]
    return [
        jnp.concatenate([part[at : at + half] for part in wide], axis=0) for at in (0, half)
    ]


def finish_kernel(
    ids_ref, slot_ref, dropped_ref, gates_ref, out_grad_ref, *refs, exp_local
):
    parts, (mixed_ref, tok_grad_ref, gate_grad_ref) = refs[:-3], refs[-3:]
    returned, returned_grad = [rows.astype(jnp.bfloat16) for rows in stack_halves(parts)]
    masks = slot_masks(ids_ref, slot_ref, dropped_ref, exp_local, returned.shape[0])
    select = sum(mask.astype(jnp.float32) for mask in masks).astype(jnp.bfloat16)
    tok_grad_ref[...] = contract(select, returned_grad, 0, 0).astype(jnp.bfloat16)
    tokens = gates_ref.shape[1]
    gates = jnp.concatenate([gates_ref[...], jnp.zeros((6, tokens), jnp.float32)], axis=0).T
    wide = out_grad_ref[...].astype(jnp.float32)
    mixed = jnp.zeros(wide.shape, jnp.float32)
    grads = []
    for k, mask in enumerate(masks):
        picked = contract(mask.astype(jnp.bfloat16), returned, 0, 0)
        mixed = mixed + gates[:, k : k + 1] * picked
        grads.append(jnp.sum(picked * wide, axis=1, keepdims=True))
    mixed_ref[...] = mixed.astype(jnp.bfloat16)
    grads.append(jnp.zeros((tokens, 6), jnp.float32))
    gate_grad_ref[...] = jnp.concatenate(grads, axis=1).T[:2]


def split_kernel(after_ref, *refs, exp_local):
    for out_ref, rows in zip(refs[-2:], stack_halves(refs[:-2])):
        order = order_matrix(exp_local, rows.shape[0])
        out_ref[...] = contract(order, rows.astype(jnp.bfloat16), 1, 0).astype(jnp.bfloat16)


def pair_kernel(*refs):
    own_ref, mate_ref, out_ref = refs[-3:]
    half = own_ref.shape[0]
    out_ref[:half] = own_ref[...]
    out_ref[half:] = mate_ref[...]


def pass_kernel(*refs):
    refs[-1][...] = refs[-2][...]


def add(left_ref, right_ref):
    total = left_ref[...].astype(jnp.float32) + right_ref[...].astype(jnp.float32)
    return total.astype(jnp.bfloat16)


def add_kernel(*refs):
    left_ref, right_ref = refs[-3:-1]
    refs[-1][...] = add(left_ref, right_ref)


def add_split_kernel(*refs):
    left_ref, right_ref, mine_ref, other_ref = refs[-4:]
    half = mine_ref.shape[0]
    total = add(left_ref, right_ref)
    mine_ref[...] = total[:half]
    other_ref[...] = total[half:]


def join_kernel(*refs, groups, exp_local):
    first_a, first_b, second_a, second_b = refs[-groups - 4 : -groups]
    order = order_matrix(exp_local, first_a.shape[0])
    first = contract(order, add(first_a, first_b), 0, 0)
    second = contract(order, add(second_a, second_b), 0, 0)
    half = first.shape[0] // groups
    for group, out_ref in enumerate(refs[-groups:]):
        part = slice(group * half, (group + 1) * half)
        out_ref[...] = jnp.concatenate([first[part], second[part]], axis=0).astype(jnp.bfloat16)


def hold_kernel(*refs):
    weight_ref, held_ref, done_ref, sems = refs[-4:]
    copies = [
        pltpu.make_async_copy(weight_ref.at[x], held_ref.at[x], sems.at[x])
        for x in range(weight_ref.shape[0])
    ]
    for copy in copies:
        copy.start()
    done_ref[...] = jnp.zeros(done_ref.shape, done_ref.dtype)
    for copy in copies:
        copy.wait()


def w_out_grad_kernel(*refs, skip, expert, at, chunk):
    hidden_ref, rows_ref = refs[skip : skip + 2]
    out_ref, done_ref, made, sems = refs[-4:]
    done_ref[...] = jnp.zeros(done_ref.shape, done_ref.dtype)
    copies = []
    for i, begin in enumerate(range(0, made.shape[0], chunk)):
        here, there = pl.ds(begin, chunk), pl.ds(at + begin, chunk)
        made[here] = contract(hidden_ref[expert, :, there], rows_ref[expert], 0, 0)
        copies.append(
            pltpu.make_async_copy(made.at[here], out_ref.at[expert, there], sems.at[i])
        )
        copies[-1].start()
    for copy in copies:
        copy.wait()


def w_in_grad_kernel(*refs, skip, expert, at, chunk):
    pre_grad_ref, rows_ref = refs[skip : skip + 2]
    out_ref, done_ref, made, sems = refs[-4:]
    done_ref[...] = jnp.zeros(done_ref.shape, done_ref.dtype)
    width, units = made.shape
    copies = []
    for i, begin in enumerate(range(0, width, chunk)):
        here = pl.ds(begin, min(chunk, width - begin))
        turned = rows_ref[expert, :, here].T
        made[here] = contract(turned, pre_grad_ref[expert, :, at : at + units], 1, 0)
        there = out_ref.at[expert, here, pl.ds(at, units)]
        copies.append(pltpu.make_async_copy(made.at[here], there, sems.at[i]))
        copies[-1].start()
    for copy in copies:
        copy.wait()


def params(rows):
    return pltpu.CompilerParams(vmem_limit_bytes=(6 << 20) + rows * (24 << 10))


def prepare(choices, gates, tokens, out_grad, groups, exp_local):
    block = (2 * exp_local * CAP, tokens.shape[1])
    whole = pl.BlockSpec(memory_space=pltpu.VMEM)
    return pl.pallas_call(
        functools.partial(prepare_kernel, exp_local=exp_local),
        out_specs=[whole] * groups,
        out_shape=[pltpu.VMEM(block, jnp.bfloat16)]
        + [jax.ShapeDtypeStruct(block, jnp.bfloat16)] * (groups - 1),
        compiler_params=pltpu.CompilerParams(vmem_limit_bytes=60 << 20),
        name="prepare",
    )(*choices, gates, tokens, out_grad)


def finish(choices, gates, out_grad, parts, exp_local):
    return pl.pallas_call(
        functools.partial(finish_kernel, exp_local=exp_local),
        out_shape=[
            jax.ShapeDtypeStruct(out_grad.shape, jnp.bfloat16),
            jax.ShapeDtypeStruct(out_grad.shape, jnp.bfloat16),
            jax.ShapeDtypeStruct(gates.shape, jnp.float32),
        ],
        compiler_params=params(out_grad.shape[0]),
        name="finish",
    )(*choices, gates, out_grad, *parts)


def small_call(kernel, name, after, operands, counts):
    width = operands[0].shape[1]
    results = pl.pallas_call(
        kernel,
        in_specs=[pl.BlockSpec(memory_space=pl.ANY)] * len(after)
        + [pl.BlockSpec(memory_space=pltpu.VMEM)] * len(operands),
        out_shape=[jax.ShapeDtypeStruct((count, width), jnp.bfloat16) for count in counts],
        compiler_params=params(4 * counts[0]),
        cost_estimate=order_cost(counts[0], width),
        name=name,
    )(*after, *operands)
    return list(results)


def hold(after, weight):
    return pl.pallas_call(
        hold_kernel,
        in_specs=[pl.BlockSpec(memory_space=pl.ANY)] * (len(after) + 1),
        out_specs=[pl.BlockSpec(memory_space=pltpu.VMEM)] * 2,
        out_shape=[pltpu.VMEM(weight.shape, weight.dtype), DONE],
        scratch_shapes=[pltpu.SemaphoreType.DMA((weight.shape[0],))],
        compiler_params=pltpu.CompilerParams(vmem_limit_bytes=42 << 20),
        cost_estimate=pl.CostEstimate(
            flops=0, bytes_accessed=4 * weight.size, transcendentals=0
        ),
        name="hold",
    )(*after, weight)


def weight_gradient(kernel, hidden, rows, shape, after, name, expert, part, parts, base=None):
    whole = pl.BlockSpec(memory_space=pltpu.VMEM)
    anywhere = pl.BlockSpec(memory_space=pl.ANY)
    width, units = rows.shape[2], hidden.shape[2] // parts
    made, chunk = (width, units), CHUNK
    if kernel is w_out_grad_kernel:
        made, chunk = (units, width), min(CHUNK // 2, units)
    operands = (*after, hidden, rows) + (() if base is None else (base,))
    return pl.pallas_call(
        functools.partial(kernel, skip=len(after), expert=expert, at=part * units, chunk=chunk),
        in_specs=[anywhere] * len(after) + [whole] * 2 + [anywhere] * (base is not None),
        out_specs=[anywhere, whole],
        out_shape=[jax.ShapeDtypeStruct(shape, jnp.float32), DONE],
        input_output_aliases={} if base is None else {len(operands) - 1: 0},
        scratch_shapes=[
            pltpu.VMEM(made, jnp.float32),
            pltpu.SemaphoreType.DMA((-(-made[0] // chunk),)),
        ],
        compiler_params=pltpu.CompilerParams(vmem_limit_bytes=24 << 20),
        cost_estimate=pl.CostEstimate(
            flops=2 * rows.shape[1] * units * width,
            bytes_accessed=4 * units * width,
            transcendentals=0,
        ),
        name=name,
    )(*operands)


def sort_kernel(after_ref, *refs, places):
    blocks, out_ref = refs[:-1], refs[-1]
    experts = out_ref.shape[0]
    part = blocks[0].shape[0] // (2 * experts)
    for i, place in enumerate(places):
        for expert in range(experts):
            at = ((i % 2) * experts + expert) * part
            out_ref[expert, place * part : (place + 1) * part] = blocks[i // 2][at : at + part]


def unsort_kernel(after_ref, in_ref, *blocks):
    experts = in_ref.shape[0]
    part = blocks[0].shape[0] // (2 * experts)
    for i in range(2 * len(blocks)):
        for expert in range(experts):
            at = ((i % 2) * experts + expert) * part
            blocks[i // 2][at : at + part] = in_ref[expert, i * part : (i + 1) * part]


def backward_kernel(after_ref, *refs, places):
    blocks, (slope_ref, w_in_ref, w_out_ref) = refs[:-7], refs[-7:-4]
    rows_ref, pre_grad_ref, row_grad_ref, turned = refs[-4:]
    experts, units, width = w_out_ref.shape
    step = min(2 * CHUNK, units)
    sort_kernel(after_ref, *blocks, rows_ref, places=places)
    for expert in range(experts):
        grads = rows_ref[expert].T
        for at in range(0, units, step):
            here = slice(at, at + step)
            hidden_grad = contract(w_out_ref[expert, here], grads, 1, 0)
            pre_grad = (hidden_grad * slope_ref[expert, :, here].T).astype(jnp.bfloat16)
            turned[here] = pre_grad
            pre_grad_ref[expert, :, here] = pre_grad.T
        for at in range(0, width, CHUNK):
            here = slice(at, min(at + CHUNK, width))
            row_grad = contract(w_in_ref[expert, here], turned[...], 1, 0)
            row_grad_ref[expert, :, here] = row_grad.T.astype(jnp.bfloat16)


def order_cost(count, width):
    return pl.CostEstimate(
        flops=2 * count * count * width, bytes_accessed=4 * count * width, transcendentals=0
    )


def sort_rows(blocks, experts, places, after):
    count, width = blocks[0].shape
    rows = len(blocks) * count // experts
    return pl.pallas_call(
        functools.partial(sort_kernel, places=places),
        in_specs=[pl.BlockSpec(memory_space=pl.ANY)]
        + [pl.BlockSpec(memory_space=pltpu.VMEM)] * len(blocks),
        out_shape=jax.ShapeDtypeStruct((experts, rows, width), jnp.bfloat16),
        compiler_params=params(rows),
        cost_estimate=order_cost(experts * rows, width),
        name="sort_rows",
    )(after, *blocks)


def backward(blocks, slope, w_in, w_out, places, after):
    experts, units, width = w_out.shape
    rows = slope.shape[1]
    by_row = jax.ShapeDtypeStruct((experts, rows, width), jnp.bfloat16)
    return pl.pallas_call(
        functools.partial(backward_kernel, places=places),
        in_specs=[pl.BlockSpec(memory_space=pl.ANY)]
        + [pl.BlockSpec(memory_space=pltpu.VMEM)] * (len(blocks) + 3),
        out_shape=[by_row, jax.ShapeDtypeStruct(slope.shape, jnp.bfloat16), by_row],
        scratch_shapes=[pltpu.VMEM((units, rows), jnp.bfloat16)],
        compiler_params=pltpu.CompilerParams(vmem_limit_bytes=(10 << 20) + rows * (40 << 10)),
        cost_estimate=pl.CostEstimate(
            flops=4 * experts * rows * width * units,
            bytes_accessed=4 * experts * rows * width,
            transcendentals=0,
        ),
        name="backward",
    )(after, *blocks, slope, w_in, w_out)


def unsort_rows(rows, steps, after):
    experts, count, width = rows.shape
    block = experts * count // steps
    return pl.pallas_call(
        unsort_kernel,
        in_specs=[pl.BlockSpec(memory_space=pl.ANY), pl.BlockSpec(memory_space=pltpu.VMEM)],
        out_shape=[jax.ShapeDtypeStruct((block, width), jnp.bfloat16)] * steps,
        compiler_params=params(count),
        cost_estimate=order_cost(experts * count, width),
        name="unsort_rows",
    )(after, rows)


DP = ("far", "near", "pair")


def ring_mate(position, count, odd):
    if (position % 2 == 1) == odd:
        return (position + 1) % count
    return (position - 1) % count


def odd_edges(count):
    columns = count // 2
    ring = [2 * c for c in range(columns)] + [2 * c + 1 for c in reversed(range(columns))]
    return [(ring[i], ring[ring_mate(i, count, True)]) for i in range(count)]


def ring_order(count, odd):
    held = [[i, ring_mate(i, count, odd)] for i in range(count)]
    blocks = [list(pair) for pair in held]
    for _ in range(count // 2 - 1):
        odd = not odd
        held = [held[ring_mate(i, count, odd)] for i in range(count)]
        for mine, more in zip(blocks, held):
            mine += more
    return blocks


def regroup(count):
    even, odd = ring_order(count, False), ring_order(count, True)
    places = {tuple(e.index(block) for block in o) for e, o in zip(even, odd)}
    (place,) = places
    return place


def swap(block, odd):
    if odd:
        return lax.ppermute(block, DP, odd_edges(lax.axis_size(DP)))
    return lax.ppermute(block, "near", [(0, 1), (1, 0)])


def expert_swap(blocks):
    size = lax.axis_size("expert")
    got = [
        lax.ppermute(blocks[k], "expert", [(i, i ^ k) for i in range(size)])
        for k in reversed(range(1, size))
    ]
    return [blocks[0]] + got[::-1]


def per_device(tokens, expert_ids, slot_ids, dropped, gates, w_in, w_out, out_grad):
    n_expert = lax.axis_size("expert")
    n_dp = lax.axis_size(DP)
    steps = n_dp // 2
    exp_local = w_in.shape[0]
    count = n_expert * exp_local * CAP
    choices = (expert_ids.T, slot_ids.T, dropped.T)
    gates = gates.T
    send = prepare(choices, gates, tokens, out_grad, n_expert, exp_local)
    got = expert_swap(send)
    held_in, done_in = hold([], w_in)
    own_rows, own_grads = small_call(
        functools.partial(split_kernel, exp_local=exp_local), "split", [done_in], got, [count] * 2
    )

    mate_rows, mate_grads = swap(own_rows, False), swap(own_grads, True)
    pairs = [own_rows, mate_rows]
    row_blocks = small_call(pair_kernel, "pair", [mate_grads], pairs, [2 * count])
    pairs = [own_grads, mate_grads]
    grad_blocks = small_call(pair_kernel, "pair", [], pairs, [2 * count])
    held_out, done_out = hold([row_blocks[0], grad_blocks[0]], w_out)
    for step in range(1, steps):
        arrived = swap(row_blocks[-1], step % 2 == 1)
        if step == 1:
            (arrived,) = small_call(pass_kernel, "pass", [done_out], [arrived], [2 * count])
        row_blocks.append(arrived)
        grad_blocks.append(swap(grad_blocks[-1], step % 2 == 0))
    rows = sort_rows(row_blocks, exp_local, range(n_dp), done_in)
    pre = jnp.einsum("xmd,xdf->xmf", rows, held_in, preferred_element_type=jnp.float32)
    hidden = gelu_exact(pre).astype(jnp.bfloat16)
    output = jnp.einsum("xmf,xfd->xmd", hidden, held_out, preferred_element_type=jnp.float32)
    out_blocks = unsort_rows(output.astype(jnp.bfloat16), steps, done_out)
    grad_rows, pre_grad, row_grad = backward(
        grad_blocks, gelu_slope(pre), held_in, held_out, regroup(n_dp), out_blocks[-1]
    )
    back_blocks = unsort_rows(row_grad, steps, done_out)

    def out_piece(expert, part, parts):
        return (w_out_grad_kernel, hidden, grad_rows, w_out.shape, expert, part, parts)

    def in_piece(expert, part, parts):
        return (w_in_grad_kernel, pre_grad, rows, w_in.shape, expert, part, parts)

    work = []
    for expert in range(exp_local):
        work += [out_piece(expert, 0, 1), in_piece(expert, 0, 1)]
    made = {}

    def next_piece(*after):
        if len(work) == 0:
            return after[0]
        kernel, left, right, shape, expert, part, parts = work.pop(0)
        name = kernel.__name__
        made[name], ready = weight_gradient(
            kernel, left, right, shape, after, name, expert, part, parts, made.get(name)
        )
        return ready

    def add_step(after, block, arrived, step):
        if step > 1:
            return small_call(add_kernel, "add", after, [block, arrived], [2 * count])
        return small_call(add_split_kernel, "add_split", after, [block, arrived], [count] * 2)

    last = steps - 1
    out_sum = out_blocks[last:]
    out_arrived = swap(out_sum[0], last % 2 == 1)
    for step in range(last, 0, -1):
        if step < last:
            back_arrived = swap(back_sum[-1], step % 2 == 1)
        ready = [next_piece(back_sum[-1])] if step == 1 < last else []
        out_sum = add_step(ready, out_blocks[step - 1], out_arrived, step)
        out_arrived = swap(out_sum[-1], step % 2 == 0)
        if step == last:
            back_sum = back_blocks[last:]
            back_arrived = swap(back_sum[-1], step % 2 == 1)
            ready = [next_piece(back_sum[-1], out_sum[-1])]
        back_sum = add_step(ready, back_blocks[step - 1], back_arrived, step)
    back_arrived = swap(back_sum[-1], False)
    joined = small_call(
        functools.partial(join_kernel, groups=n_expert, exp_local=exp_local),
        "join",
        [next_piece(back_sum[-1])],
        [out_sum[0], out_arrived, back_sum[0], back_arrived],
        [2 * exp_local * CAP] * n_expert,
    )
    while work:
        next_piece(joined[0])
    mixed, tok_grad, gate_grad = finish(
        choices, gates, out_grad, expert_swap(joined), exp_local
    )
    return (mixed, tok_grad, gate_grad.T, made["w_in_grad_kernel"], made["w_out_grad_kernel"])


def solution(mesh):
    n_expert, n_dp = mesh.shape["expert"], mesh.shape["dp"]
    split = Mesh(mesh.devices.reshape(n_expert, n_dp // 4, 2, 2), ("expert",) + DP)
    rows = P(("expert",) + DP, None)
    into = P("expert", None, DP)
    out_of = P("expert", DP, None)
    return jax.shard_map(
        per_device,
        mesh=split,
        in_specs=(rows, rows, rows, rows, rows, into, out_of, rows),
        out_specs=(rows, rows, rows, into, out_of),
        check_vma=False,
    )
```
